32 devices in a mesh: groups: 2 (over y), patch: 8 (over z, x), head: 2 (over core).
Axes of the slice: x: 2, y: 2, z: 4, core: 2. Of those that a mesh axis runs over, the one named last changes fastest.
Arguments:
- queries: bfloat16 [2, 256, 1536], P(None, ('groups', 'patch'), 'head'), parts along dimension 1, may hold values from -15 to 15
- stale_pairs: bfloat16 [2, 320, 1536], P(None, ('groups', 'patch'), 'head'), parts along dimension 1, may hold values from -6 to 6
- step_pairs: bfloat16 [2, 2, 320, 1536], P(None, None, ('groups', 'patch'), 'head'), parts along dimension 2, may hold values from -6 to 6
- hidden: bfloat16 [256, 3072], P(('groups', 'patch'), 'head'), parts along dimension 0, may hold values from -3 to 3
- out_weight: bfloat16 [1536, 3072], P('head'), may hold values from -0.15625 to 0.15625
- gate_table: bfloat16 [28, 3072], replicated, may hold values from -4 to 4
- t_index: int32 [4], P('groups'), parts along dimension 0, may hold values from 0 to 27
- text_len: int32 [2], P('groups'), parts along dimension 0, may hold values from 1 to 32
Outputs:
- final_latents: bfloat16 [256, 3072], P(('groups', 'patch', 'head')), parts along dimension 0
The draws below stay inside these ranges and needn't reach their ends.
There are 2 independent parts, one for each index of `groups`. The reference program is written for one: setup_inputs(seed, part) draws one part's arguments, and reference() takes and returns one part's arrays. A program takes and returns all parts, laid end to end along the dimension named above; an argument that names none is the same for every part. Nothing has to cross between parts.
All inputs are finite; a program needn't handle non-finite values.
Results may differ from the reference program's by a relative error of at most 0.0065.
Values may be sent and summed in bfloat16 or wider, within the bound.
No kernel may reach another device: no remote copies, remote signals or barrier semaphores. Data moves between devices by JAX's collectives and lax.ppermute only.
A program may use at most 128 MiB of HBM per device.

```python
import jax
import jax.numpy as jnp
from jax import lax

D = 3072
HEADS = 12
HDIM = 128
LAT_DEV = 16
TXT_DEV = 4
NSCHED = 28
ROWS = 20
LAT = 128
TXT = 32
SEQ = 160
HD = 1536
N_PATCH = 8


def joint_draw(key):
    base = jax.random.fold_in(key, 7)
    key_query, key_stale, key_fresh = jax.random.split(base, 3)
    queries = 2.5 * jax.random.truncated_normal(key_query, -6.0, 6.0, (2, LAT, HD), jnp.float32)
    stale = jax.random.truncated_normal(key_stale, -6.0, 6.0, (2, SEQ, HD), jnp.float32)
    fresh = jax.random.truncated_normal(key_fresh, -6.0, 6.0, (2, 2, SEQ, HD), jnp.float32)
    return (queries, stale, fresh)


def draw_queries(key, part):
    return joint_draw(key)[0].astype(jnp.bfloat16)


def draw_stale_pairs(key, part):
    return joint_draw(key)[1].astype(jnp.bfloat16)


def draw_step_pairs(key, part):
    return joint_draw(key)[2].astype(jnp.bfloat16)


def levels(key, shape, pieces, least, top_value):
    def one(position, shards_of):
        heights = jax.random.uniform(jax.random.fold_in(jax.random.fold_in(key, 6), position), (shards_of,), jnp.float32, least / len(pieces), top_value / len(pieces))
        return jnp.repeat(jnp.exp(heights), shape[position] // shards_of).reshape((-1,) + (1,) * (len(shape) - position - 1))

    gain = one(*pieces[0])
    for cut in pieces[1:]:
        gain = gain * one(*cut)
    return gain


def noise(rng, shape, width, bound, cuts=(), held_as=jnp.bfloat16):
    factor_of = levels(rng, shape, cuts, -0.22, 0.18) if cuts else 1.0
    entries = jax.random.normal(rng, shape, jnp.float32) * width * factor_of
    return jnp.minimum(jnp.maximum(entries, -bound), bound).astype(held_as)


def setup_inputs(seed: int = 0, part: int = 0) -> dict:
    splits = jax.random.split(jax.random.key(seed), 9)
    part_splits = jax.random.split(jax.random.fold_in(splits[8], part), 9)
    return {
        "queries": draw_queries(jax.random.fold_in(jax.random.fold_in(splits[8], part), 71), part),
        "stale_pairs": draw_stale_pairs(jax.random.fold_in(jax.random.fold_in(splits[8], part), 71), part),
        "step_pairs": draw_step_pairs(jax.random.fold_in(jax.random.fold_in(splits[8], part), 71), part),
        "hidden": noise(part_splits[3], (LAT, D), 0.5, 3.0, ((0, 8), (1, 2))),
        "out_weight": noise(splits[4], (HD, D), HD ** -0.5, 0.15625, ((0, 2),)),
        "gate_table": noise(splits[5], (NSCHED, D), 1.0, 4.0),
        "t_index": jax.random.randint(part_splits[6], (2,), 0, NSCHED).astype(jnp.int32),
        "text_len": jax.random.randint(part_splits[7], (1,), 1, TXT + 1).astype(jnp.int32),
    }


def attend(query_rows, key_rows, value_rows, usable):
    count = query_rows.shape[0]
    total = key_rows.shape[0]
    qf = query_rows.reshape(count, HEADS, HDIM).astype(jnp.float32)
    kf = key_rows.reshape(total, HEADS, HDIM).astype(jnp.float32)
    vf = value_rows.reshape(total, HEADS, HDIM).astype(jnp.float32)
    scores = jnp.einsum("qhd,khd->hqk", qf, kf) * (1.0 / (HDIM ** 0.5))
    scores = jnp.where(usable[None, None, :], scores, jnp.float32(-1e30))
    top = jnp.max(scores, axis=2, keepdims=True)
    expo = jnp.exp(scores - top)
    weights = (expo / jnp.sum(expo, axis=2, keepdims=True)).astype(jnp.bfloat16)
    mixed = jnp.einsum("hqk,khd->qhd", weights.astype(jnp.float32), vf)
    return mixed.reshape(count, HEADS * HDIM).astype(jnp.bfloat16)


def reference(queries, stale_pairs, step_pairs, hidden, out_weight, gate_table, t_index, text_len):
    positions = jnp.arange(SEQ, dtype=jnp.int32)
    within = positions % ROWS
    holder = positions // ROWS
    usable = (within < LAT_DEV) | (holder * TXT_DEV + within - LAT_DEV < text_len[0])
    state = hidden.astype(jnp.float32)
    remote_sets = (stale_pairs, step_pairs[0])
    for section in range(2):
        remote = remote_sets[section]
        fresh = step_pairs[section]
        section_queries = queries[section]

        def one_strip(strip_index):
            start = (strip_index * ROWS).astype(jnp.int32)
            own = lax.dynamic_slice_in_dim(fresh, start, ROWS, axis=1)
            pairs = lax.dynamic_update_slice_in_dim(remote, own, start, axis=1)
            qstart = (strip_index * LAT_DEV).astype(jnp.int32)
            query_rows = lax.dynamic_slice_in_dim(section_queries, qstart, LAT_DEV, axis=0)
            return attend(query_rows, pairs[0], pairs[1], usable)

        attended = lax.map(one_strip, jnp.arange(N_PATCH, dtype=jnp.int32)).reshape(LAT, HD)
        projected = jnp.dot(attended, out_weight, preferred_element_type=jnp.float32)
        gate_row = gate_table[t_index[section]].astype(jnp.float32)
        state = state + gate_row[None, :] * projected
    return state.astype(jnp.bfloat16)
```

```python
import functools

import jax
import jax.numpy as jnp
import numpy as np
from jax import lax
from jax.experimental import pallas as pl
from jax.experimental.pallas import tpu as pltpu
from jax.sharding import PartitionSpec as P

HDIM = 128
LANES = 128
TILE = 16
MASKED = -1e30
VMEM_LIMIT = 24 * 1024 * 1024


def round_up(value, step):
    return (value + step - 1) // step * step


def attention_kernel(sizes, bias_ref, own_ref, local_ref, pair_ref, *refs):
    set_rows, query_rows, columns = sizes
    others, (mine_ref, back_ref) = refs[:-2], refs[-2:]
    pair_rows = 2 * set_rows
    fresh_at = query_rows
    heads = own_ref.shape[1] // HDIM
    scale = 1.0 / HDIM**0.5
    per_class = query_rows // 2
    bias = jnp.concatenate(
        [jnp.broadcast_to(bias_ref[c : c + 1, :], (per_class, columns)) for c in range(4)], axis=0
    )
    for head in range(heads):
        lanes = slice(head * HDIM, (head + 1) * HDIM)
        rows = [own_ref[:, lanes], pair_ref[:pair_rows, lanes]]
        rows += [ref[:, lanes] for ref in others]
        rows += [local_ref[fresh_at:, lanes], pair_ref[pair_rows + fresh_at :, lanes]]
        filled = sum(r.shape[0] for r in rows)
        if filled < columns:
            rows.append(jnp.zeros((columns - filled, HDIM), jnp.bfloat16))
        keys = jnp.concatenate(rows, axis=0)
        queries = jnp.concatenate(
            [local_ref[:fresh_at, lanes], pair_ref[pair_rows : pair_rows + fresh_at, lanes]], axis=0
        )
        scores = lax.dot_general(
            queries, keys, (((1,), (1,)), ((), ())), preferred_element_type=jnp.float32
        )
        scores = scores * scale + bias
        top = jnp.max(scores, axis=1, keepdims=True)
        expo = jnp.exp(scores - top)
        weights = expo / jnp.sum(expo, axis=1, keepdims=True)
        weights = pltpu.roll(weights, 1, 1).astype(jnp.bfloat16)
        mixed = jnp.dot(weights, keys, preferred_element_type=jnp.float32).astype(jnp.bfloat16)
        mine_ref[:, lanes] = mixed[:query_rows]
        back_ref[:, lanes] = mixed[query_rows:]


def gated(attended, weight, gates):
    strip = attended.shape[0] // 2
    projected = jnp.dot(attended, weight, preferred_element_type=jnp.float32)
    return gates[0:1, :] * projected[:strip] + gates[1:2, :] * projected[strip:]


def first_half_kernel(place_ref, attended_ref, weight_ref, gates_ref, hidden_ref, out_ref):
    depth = attended_ref.shape[1]
    width = hidden_ref.shape[1]
    rows = pl.ds(pl.multiple_of(place_ref[0] * depth, depth), depth)
    out_ref[...] = gated(attended_ref[...], weight_ref[rows, :], gates_ref[...])
    lanes = pl.ds(pl.multiple_of(place_ref[1] * width, LANES), width)
    out_ref[:, lanes] += hidden_ref[...].astype(jnp.float32)


def second_half_kernel(place_ref, attended_ref, weight_ref, gates_ref, sum_ref, keep_ref, send_ref, total):
    depth = attended_ref.shape[1]
    half = keep_ref.shape[0]
    rows = pl.ds(pl.multiple_of((1 - place_ref[0]) * depth, depth), depth)
    total[...] = sum_ref[...] + gated(attended_ref[...], weight_ref[rows, :], gates_ref[...])
    core = place_ref[1]
    keep_ref[...] = total[pl.ds(pl.multiple_of(core * half, half), half), :]
    send_ref[...] = total[pl.ds(pl.multiple_of((1 - core) * half, half), half), :].astype(jnp.bfloat16)


def per_device(queries, stale_pairs, step_pairs, hidden, out_weight, gate_table, t_index, text_len):
    strips = lax.axis_size("patch")
    strip = lax.axis_index("patch")
    core = lax.axis_index("head")
    strip_rows = stale_pairs.shape[1]
    lat_rows = queries.shape[1]
    text_rows = strip_rows - lat_rows
    width = queries.shape[2]
    half = width // 2
    side = strip % 2
    set_rows = 2 * strip_rows
    query_rows = 2 * lat_rows

    def interleaved(pairs):
        return pairs.transpose(1, 0, 2).reshape(set_rows, width)

    def near(rows):
        return jnp.where(side == 0, rows[:, :half], rows[:, half:])

    def far(rows):
        return jnp.where(side == 0, rows[:, half:], rows[:, :half])

    remote = jnp.concatenate([interleaved(stale_pairs), interleaved(step_pairs[0])], axis=0)
    extra = jnp.concatenate([queries.reshape(query_rows, width), interleaved(step_pairs[1])], axis=0)

    def to(rows, flip):
        return lax.ppermute(rows, "patch", [(i, i ^ flip) for i in range(strips)])

    own, other = near(remote), far(remote)
    local = near(extra)
    held = {0: own}
    bit = strips // 2
    pair = None
    while bit > 1:
        arrived = {bit: to(own, bit), bit + 1: to(other, bit + 1)}
        if pair is None:
            pair = to(jnp.concatenate([other, far(extra)], axis=0), 1)
        for flip, block in held.items():
            if flip > 1:
                arrived[flip + bit] = to(block, bit)
        held.update(arrived)
        bit //= 2
    flips = sorted(flip for flip in held if flip > 1)
    blocks = [0, 1] + flips

    filled = 2 * set_rows * len(blocks) + 2 * set_rows
    columns = round_up(filled, LANES)
    column = np.arange(columns)
    in_blocks = column < 2 * set_rows * len(blocks)
    block = np.minimum(column // (2 * set_rows), len(blocks) - 1)
    within = column % (2 * set_rows)
    flip = np.where(in_blocks, np.asarray(blocks)[block], within // set_rows)
    kind = np.where(in_blocks, within // set_rows, np.where(column < filled, 2, 3))
    token = (within % set_rows) // 2
    whose, step = np.asarray([0, 0, 1, 1])[:, None], np.asarray([0, 1, 0, 1])[:, None]
    wanted = np.where(flip == whose, step + 1, step)
    chosen = (within % 2 == 0) & (kind == wanted)
    holder = strip ^ jnp.asarray(flip, jnp.int32)
    live = (token < lat_rows) | (holder * text_rows + (token - lat_rows) < text_len[0])
    bias = jnp.where(chosen & live[None, :], jnp.float32(0.0), jnp.float32(MASKED))

    attended_shape = jax.ShapeDtypeStruct((query_rows, half), jnp.bfloat16)
    mine, back = pl.pallas_call(
        functools.partial(attention_kernel, (set_rows, query_rows, columns)),
        out_shape=(attended_shape, attended_shape),
        compiler_params=pltpu.CompilerParams(vmem_limit_bytes=VMEM_LIMIT),
    )(bias, own, local, pair, *[held[flip] for flip in flips])
    returned = to(back, 1)

    model = out_weight.shape[1]
    place = jnp.stack([side, core]).astype(jnp.int32)
    gates = gate_table[t_index].astype(jnp.float32)
    smem = pl.BlockSpec(memory_space=pltpu.SMEM)
    vmem = pl.BlockSpec(memory_space=pltpu.VMEM)
    partial_sum = pl.pallas_call(
        first_half_kernel,
        out_shape=jax.ShapeDtypeStruct((lat_rows, model), jnp.float32),
        in_specs=[smem, vmem, vmem, vmem, vmem],
        out_specs=vmem,
        compiler_params=pltpu.CompilerParams(vmem_limit_bytes=VMEM_LIMIT),
    )(place, mine, out_weight, gates, hidden)
    keep, send = pl.pallas_call(
        second_half_kernel,
        out_shape=(
            jax.ShapeDtypeStruct((lat_rows // 2, model), jnp.float32),
            jax.ShapeDtypeStruct((lat_rows // 2, model), jnp.bfloat16),
        ),
        in_specs=[smem, vmem, vmem, vmem, vmem],
        out_specs=(vmem, vmem),
        scratch_shapes=[pltpu.VMEM((lat_rows, model), jnp.float32)],
        compiler_params=pltpu.CompilerParams(vmem_limit_bytes=VMEM_LIMIT),
    )(place, returned, out_weight, gates, partial_sum)
    received = lax.ppermute(send, "head", [(0, 1), (1, 0)])
    return (keep + received.astype(jnp.float32)).astype(jnp.bfloat16)


def solution(mesh):
    return jax.shard_map(
        per_device,
        mesh=mesh,
        in_specs=(
            P(None, ("groups", "patch"), "head"),
            P(None, ("groups", "patch"), "head"),
            P(None, None, ("groups", "patch"), "head"),
            P(("groups", "patch"), "head"),
            P("head", None),
            P(),
            P("groups"),
            P("groups"),
        ),
        out_specs=P(("groups", "patch", "head"), None),
        check_vma=False,
    )
```

```python
import functools

import jax
import jax.numpy as jnp
import numpy as np
from jax import lax
from jax.experimental import pallas as pl
from jax.experimental.pallas import tpu as pltpu
from jax.sharding import PartitionSpec as P

HDIM = 128
LANES = 128
MASKED = -1e30
VMEM_LIMIT = 24 * 1024 * 1024


def round_up(value, step):
    return (value + step - 1) // step * step


def pack_kernel(sizes, text_hbm, table_hbm, stale_hbm, step_hbm, query_hbm, own_ref, other_ref, local_ref, pair_ref, bias_ref,
                text_ref, table_ref, stale, step, query, sems):
    strips, lat_rows, text_rows = sizes
    copies = [
        pltpu.make_async_copy(stale_hbm, stale, sems.at[0]),
        pltpu.make_async_copy(step_hbm, step, sems.at[1]),
        pltpu.make_async_copy(query_hbm, query, sems.at[2]),
        pltpu.make_async_copy(text_hbm, text_ref, sems.at[3]),
        pltpu.make_async_copy(table_hbm, table_ref, sems.at[4]),
    ]
    for copy in copies:
        copy.start()
    strip = lax.axis_index("patch")
    side = lax.rem(strip, 2)
    half = own_ref.shape[1]
    for copy in copies:
        copy.wait()
    early = table_ref[5:6, :]
    live = (early < 0) | ((strip ^ table_ref[4:5, :]) * text_rows + early < text_ref[0])
    for c in range(4):
        bias_ref[c : c + 1, :] = jnp.where((table_ref[c : c + 1, :] > 0) & live, 0.0, MASKED)

    def pick(ref, lead, which):
        lanes = pl.ds(pl.multiple_of(which * half, LANES), half)
        rows = ref[lead + (slice(None),) * (len(ref.shape) - len(lead) - 1) + (lanes,)]
        return rows.reshape(-1, half)

    for which, block_ref, rest_ref in ((side, own_ref, local_ref), (1 - side, other_ref, pair_ref)):
        block = jnp.concatenate([pick(stale, (), which), pick(step, (0,), which)], axis=0)
        rest = jnp.concatenate([pick(query, (), which), pick(step, (1,), which)], axis=0)
        block_ref[...] = block
        if rest_ref is pair_ref:
            rest = jnp.concatenate([block, rest], axis=0)
        spare = rest_ref.shape[0] - rest.shape[0]
        rest_ref[...] = jnp.concatenate([rest, jnp.zeros((spare, half), rest.dtype)], axis=0) if spare else rest


def attention_kernel(sizes, bias_ref, own_ref, local_ref, pair_ref, *refs):
    set_rows, query_rows, columns = sizes
    others, (mine_ref, back_ref) = refs[:-2], refs[-2:]
    pair_rows = 2 * set_rows
    per_class = query_rows // 2
    scale = 1.0 / HDIM**0.5
    bias = jnp.concatenate(
        [jnp.broadcast_to(bias_ref[c : c + 1, :], (per_class, columns)) for c in range(4)], axis=0
    )
    for head in range(own_ref.shape[1] // HDIM):
        lanes = slice(head * HDIM, (head + 1) * HDIM)
        rows = [own_ref[:, lanes], pair_ref[:pair_rows, lanes]]
        rows += [ref[:, lanes] for ref in others]
        rows += [local_ref[query_rows:, lanes], pair_ref[pair_rows + query_rows :, lanes]]
        filled = sum(r.shape[0] for r in rows)
        if filled < columns:
            rows.append(jnp.zeros((columns - filled, HDIM), jnp.bfloat16))
        keys = jnp.concatenate(rows, axis=0)
        queries = jnp.concatenate(
            [local_ref[:query_rows, lanes], pair_ref[pair_rows : pair_rows + query_rows, lanes]], axis=0
        )
        scores = lax.dot_general(
            queries, keys, (((1,), (1,)), ((), ())), preferred_element_type=jnp.float32
        )
        scores = scores * scale + bias
        top = jnp.max(scores, axis=1, keepdims=True)
        expo = jnp.exp(scores - top)
        weights = expo / jnp.sum(expo, axis=1, keepdims=True)
        weights = pltpu.roll(weights, 1, 1).astype(jnp.bfloat16)
        mixed = jnp.dot(weights, keys, preferred_element_type=jnp.float32).astype(jnp.bfloat16)
        mine_ref[:, lanes] = mixed[:query_rows]
        back_ref[:, lanes] = mixed[query_rows:]


def gated(attended, weight, gates):
    strip = attended.shape[0] // 2
    projected = jnp.dot(attended, weight, preferred_element_type=jnp.float32)
    return gates[0:1, :] * projected[:strip] + gates[1:2, :] * projected[strip:]


def first_half_kernel(attended_ref, plan_hbm, table_hbm, hidden_hbm, weight_hbm, sum_ref, gates_ref, far_ref,
                      plan_ref, table_ref, hidden_ref, near, sems):
    depth = attended_ref.shape[1]
    width = hidden_ref.shape[1]
    side = lax.rem(lax.axis_index("patch"), 2)
    rows = pl.ds(pl.multiple_of(side * depth, depth), depth)
    far_rows = pl.ds(pl.multiple_of((1 - side) * depth, depth), depth)
    near_copy = pltpu.make_async_copy(weight_hbm.at[rows, :], near, sems.at[0])
    far_copy = pltpu.make_async_copy(weight_hbm.at[far_rows, :], far_ref, sems.at[1])
    small = [
        pltpu.make_async_copy(plan_hbm, plan_ref, sems.at[2]),
        pltpu.make_async_copy(table_hbm, table_ref, sems.at[3]),
        pltpu.make_async_copy(hidden_hbm, hidden_ref, sems.at[4]),
    ]
    for copy in small + [near_copy, far_copy]:
        copy.start()
    for copy in small:
        copy.wait()
    table = table_ref[...].astype(jnp.float32)
    entry = lax.broadcasted_iota(jnp.int32, table.shape, 0)
    for step in range(2):
        row = jnp.sum(jnp.where(entry == plan_ref[step], table, 0.0), axis=0, keepdims=True)
        gates_ref[step : step + 1, :] = row
    near_copy.wait()
    sum_ref[...] = gated(attended_ref[...], near[...], gates_ref[...])
    lanes = pl.ds(pl.multiple_of(lax.axis_index("head") * width, LANES), width)
    sum_ref[:, lanes] += hidden_ref[...].astype(jnp.float32)
    far_copy.wait()


def second_half_kernel(attended_ref, weight_ref, gates_ref, sum_ref, keep_ref, send_ref, total):
    half = keep_ref.shape[0]
    total[...] = sum_ref[...] + gated(attended_ref[...], weight_ref[...], gates_ref[...])
    core = lax.axis_index("head")
    keep_ref[...] = total[pl.ds(pl.multiple_of(core * half, half), half), :]
    send_ref[...] = total[pl.ds(pl.multiple_of((1 - core) * half, half), half), :].astype(jnp.bfloat16)


def per_device(queries, stale_pairs, step_pairs, hidden, out_weight, gate_table, t_index, text_len):
    strips = lax.axis_size("patch")
    strip_rows = stale_pairs.shape[1]
    lat_rows = queries.shape[1]
    text_rows = strip_rows - lat_rows
    width = queries.shape[2]
    half = width // 2
    set_rows = 2 * strip_rows
    query_rows = 2 * lat_rows
    block_rows = 2 * set_rows
    vmem = pl.BlockSpec(memory_space=pltpu.VMEM)
    hbm = pl.BlockSpec(memory_space=pltpu.HBM)
    params = pltpu.CompilerParams(vmem_limit_bytes=VMEM_LIMIT)

    def in_hbm(*arrays):
        return [pltpu.with_memory_space_constraint(array, pltpu.HBM) for array in arrays]

    flips = list(range(2, strips))
    blocks = [0, 1] + flips
    filled = block_rows * len(blocks) + 2 * set_rows
    columns = round_up(filled, LANES)
    column = np.arange(columns)
    in_blocks = column < block_rows * len(blocks)
    block = np.minimum(column // block_rows, len(blocks) - 1)
    within = column % block_rows
    flip = np.where(in_blocks, np.asarray(blocks)[block], within // set_rows)
    kind = np.where(in_blocks, within // set_rows, np.where(column < filled, 2, 3))
    token = (within % set_rows) // 2
    whose, step = np.asarray([0, 0, 1, 1])[:, None], np.asarray([0, 1, 0, 1])[:, None]
    chosen = (within % 2 == 0) & (kind == np.where(flip == whose, step + 1, step))
    unused = np.zeros((2, columns))
    table = np.concatenate([chosen, flip[None], (token - lat_rows)[None], unused], axis=0).astype(np.int32)

    bf16 = functools.partial(jax.ShapeDtypeStruct, dtype=jnp.bfloat16)
    f32 = functools.partial(jax.ShapeDtypeStruct, dtype=jnp.float32)
    local_rows = query_rows + set_rows
    own, other, local, pair, bias = pl.pallas_call(
        functools.partial(pack_kernel, (strips, lat_rows, text_rows)),
        out_shape=(
            bf16((block_rows, half)),
            bf16((block_rows, half)),
            bf16((local_rows, half)),
            bf16((block_rows + local_rows, half)),
            f32((4, columns)),
        ),
        in_specs=[hbm] * 5,
        out_specs=(vmem,) * 5,
        scratch_shapes=[
            pltpu.SMEM(text_len.shape, jnp.int32),
            pltpu.VMEM(table.shape, jnp.int32),
            pltpu.VMEM((strip_rows, 2, width), jnp.bfloat16),
            pltpu.VMEM((2, strip_rows, 2, width), jnp.bfloat16),
            pltpu.VMEM((2, lat_rows, width), jnp.bfloat16),
            pltpu.SemaphoreType.DMA((5,)),
        ],
        compiler_params=params,
    )(text_len, *in_hbm(jnp.asarray(table), stale_pairs.transpose(1, 0, 2), step_pairs.transpose(0, 2, 1, 3), queries))

    def to(rows, flip):
        return lax.ppermute(rows, "patch", [(i, i ^ flip) for i in range(strips)])

    held = {0: own}
    bit = strips // 2
    pair_rows = None
    while bit > 1:
        arrived = {bit: to(own, bit), bit + 1: to(other, bit + 1)}
        if pair_rows is None:
            pair_rows = to(pair, 1)
        for flip, rows in held.items():
            if flip > 1:
                arrived[flip + bit] = to(rows, bit)
        held.update(arrived)
        bit //= 2

    mine, back = pl.pallas_call(
        functools.partial(attention_kernel, (set_rows, query_rows, columns)),
        out_shape=(bf16((query_rows, half)),) * 2,
        compiler_params=params,
    )(bias, own, local, pair_rows, *[held[flip] for flip in flips])
    returned = to(back, 1)

    model = out_weight.shape[1]
    total, gates, far_weight = pl.pallas_call(
        first_half_kernel,
        out_shape=(f32((lat_rows, model)), f32((2, model)), bf16((half, model))),
        in_specs=[vmem] + [hbm] * 4,
        out_specs=(vmem,) * 3,
        scratch_shapes=[
            pltpu.SMEM(t_index.shape, jnp.int32),
            pltpu.VMEM(gate_table.shape, jnp.bfloat16),
            pltpu.VMEM(hidden.shape, jnp.bfloat16),
            pltpu.VMEM((half, model), jnp.bfloat16),
            pltpu.SemaphoreType.DMA((5,)),
        ],
        compiler_params=params,
    )(mine, *in_hbm(t_index, gate_table, hidden, out_weight))
    keep, send = pl.pallas_call(
        second_half_kernel,
        out_shape=(f32((lat_rows // 2, model)), bf16((lat_rows // 2, model))),
        in_specs=[vmem] * 4,
        out_specs=(vmem, vmem),
        scratch_shapes=[pltpu.VMEM((lat_rows, model), jnp.float32)],
        compiler_params=params,
    )(returned, far_weight, gates, total)
    received = lax.ppermute(send, "head", [(0, 1), (1, 0)])
    return (keep + received.astype(jnp.float32)).astype(jnp.bfloat16)


def solution(mesh):
    return jax.shard_map(
        per_device,
        mesh=mesh,
        in_specs=(
            P(None, ("groups", "patch"), "head"),
            P(None, ("groups", "patch"), "head"),
            P(None, None, ("groups", "patch"), "head"),
            P(("groups", "patch"), "head"),
            P("head", None),
            P(),
            P("groups"),
            P("groups"),
        ),
        out_specs=P(("groups", "patch", "head"), None),
        check_vma=False,
    )
```

```python
import functools

import jax
import jax.numpy as jnp
import numpy as np
from jax import lax
from jax.experimental import pallas as pl
from jax.experimental.pallas import tpu as pltpu
from jax.sharding import PartitionSpec as P

HDIM = 128
LANES = 128
MASKED = -1e30
VMEM_LIMIT = 24 * 1024 * 1024


def round_up(value, step):
    return (value + step - 1) // step * step


def pack_kernel(sizes, table_hbm, stale_hbm, step_hbm, query_hbm, own_ref, other_ref, local_ref, pair_ref, mask_ref,
                table_ref, stale, step, query, sems):
    text_rows = sizes
    copies = [
        pltpu.make_async_copy(stale_hbm, stale, sems.at[0]),
        pltpu.make_async_copy(step_hbm, step, sems.at[1]),
        pltpu.make_async_copy(query_hbm, query, sems.at[2]),
        pltpu.make_async_copy(table_hbm, table_ref, sems.at[3]),
    ]
    for copy in copies:
        copy.start()
    strip = lax.axis_index("patch")
    side = lax.rem(strip, 2)
    half = own_ref.shape[1]
    for copy in copies:
        copy.wait()
    early = table_ref[5:6, :]
    mask_ref[0:4, :] = table_ref[0:4, :]
    mask_ref[4:5, :] = jnp.where(early < 0, -1, (strip ^ table_ref[4:5, :]) * text_rows + early)

    def pick(ref, lead, which):
        lanes = pl.ds(pl.multiple_of(which * half, LANES), half)
        rows = ref[lead + (slice(None),) * (len(ref.shape) - len(lead) - 1) + (lanes,)]
        return rows.reshape(-1, half)

    for which, block_ref, rest_ref in ((side, own_ref, local_ref), (1 - side, other_ref, pair_ref)):
        block = jnp.concatenate([pick(stale, (), which), pick(step, (0,), which)], axis=0)
        rest = jnp.concatenate([pick(query, (), which), pick(step, (1,), which)], axis=0)
        block_ref[...] = block
        if rest_ref is pair_ref:
            rest = jnp.concatenate([block, rest], axis=0)
        spare = rest_ref.shape[0] - rest.shape[0]
        rest_ref[...] = jnp.concatenate([rest, jnp.zeros((spare, half), rest.dtype)], axis=0) if spare else rest


def attention_kernel(sizes, text_ref, mask_ref, own_ref, local_ref, pair_ref, *refs):
    set_rows, query_rows = sizes
    others, (mine_ref, back_ref) = refs[:-2], refs[-2:]
    pair_rows = 2 * set_rows
    columns = mask_ref.shape[1]
    scale = 1.0 / HDIM**0.5
    live = mask_ref[4:5, :] < text_ref[0]
    bias = jnp.concatenate(
        [
            jnp.broadcast_to(jnp.where((mask_ref[c : c + 1, :] > 0) & live, 0.0, MASKED), (query_rows // 2, columns))
            for c in range(4)
        ],
        axis=0,
    )
    lane_blocks = [slice(i, i + HDIM) for i in range(0, own_ref.shape[1], HDIM)]
    keys, scores = [], []
    for lanes in lane_blocks:
        rows = [own_ref[:, lanes], pair_ref[:pair_rows, lanes]]
        rows += [ref[:, lanes] for ref in others]
        rows += [local_ref[query_rows:, lanes], pair_ref[pair_rows + query_rows :, lanes]]
        filled = sum(r.shape[0] for r in rows)
        if filled < columns:
            rows.append(jnp.zeros((columns - filled, HDIM), jnp.bfloat16))
        keys.append(jnp.concatenate(rows, axis=0))
        queries = jnp.concatenate(
            [local_ref[:query_rows, lanes], pair_ref[pair_rows : pair_rows + query_rows, lanes]], axis=0
        )
        scores.append(
            lax.dot_general(queries, keys[-1], (((1,), (1,)), ((), ())), preferred_element_type=jnp.float32)
            * scale
            + bias
        )
    expos = [jnp.exp(score - jnp.max(score, axis=1, keepdims=True)) for score in scores]
    weights = [expo / jnp.sum(expo, axis=1, keepdims=True) for expo in expos]
    for lanes, weight, key in zip(lane_blocks, weights, keys):
        weight = pltpu.roll(weight, 1, 1).astype(jnp.bfloat16)
        mixed = jnp.dot(weight, key, preferred_element_type=jnp.float32).astype(jnp.bfloat16)
        mine_ref[:, lanes] = mixed[:query_rows]
        back_ref[:, lanes] = mixed[query_rows:]


def gated(attended, weight, gates):
    strip = attended.shape[0] // 2
    projected = jnp.dot(attended, weight, preferred_element_type=jnp.float32)
    return gates[0:1, :] * projected[:strip] + gates[1:2, :] * projected[strip:]


def first_half_kernel(attended_ref, plan_hbm, table_hbm, hidden_hbm, weight_hbm, sum_ref, gates_ref, far_ref,
                      plan_ref, table_ref, hidden_ref, near, sems):
    depth = attended_ref.shape[1]
    width = hidden_ref.shape[1]
    side = lax.rem(lax.axis_index("patch"), 2)
    rows = pl.ds(pl.multiple_of(side * depth, depth), depth)
    far_rows = pl.ds(pl.multiple_of((1 - side) * depth, depth), depth)
    near_copy = pltpu.make_async_copy(weight_hbm.at[rows, :], near, sems.at[0])
    far_copy = pltpu.make_async_copy(weight_hbm.at[far_rows, :], far_ref, sems.at[1])
    small = [
        pltpu.make_async_copy(plan_hbm, plan_ref, sems.at[2]),
        pltpu.make_async_copy(table_hbm, table_ref, sems.at[3]),
        pltpu.make_async_copy(hidden_hbm, hidden_ref, sems.at[4]),
    ]
    for copy in small + [near_copy, far_copy]:
        copy.start()
    for copy in small:
        copy.wait()
    table = table_ref[...].astype(jnp.float32)
    entry = lax.broadcasted_iota(jnp.int32, table.shape, 0)
    for step in range(2):
        row = jnp.sum(jnp.where(entry == plan_ref[step], table, 0.0), axis=0, keepdims=True)
        gates_ref[step : step + 1, :] = row
    near_copy.wait()
    sum_ref[...] = gated(attended_ref[...], near[...], gates_ref[...])
    lanes = pl.ds(pl.multiple_of(lax.axis_index("head") * width, LANES), width)
    sum_ref[:, lanes] += hidden_ref[...].astype(jnp.float32)
    far_copy.wait()


def second_half_kernel(attended_ref, weight_ref, gates_ref, sum_ref, keep_ref, send_ref, total):
    half = keep_ref.shape[0]
    total[...] = sum_ref[...] + gated(attended_ref[...], weight_ref[...], gates_ref[...])
    core = lax.axis_index("head")
    keep_ref[...] = total[pl.ds(pl.multiple_of(core * half, half), half), :]
    send_ref[...] = total[pl.ds(pl.multiple_of((1 - core) * half, half), half), :].astype(jnp.bfloat16)


def per_device(queries, stale_pairs, step_pairs, hidden, out_weight, gate_table, t_index, text_len):
    strips = lax.axis_size("patch")
    strip_rows = stale_pairs.shape[1]
    lat_rows = queries.shape[1]
    text_rows = strip_rows - lat_rows
    width = queries.shape[2]
    half = width // 2
    set_rows = 2 * strip_rows
    query_rows = 2 * lat_rows
    block_rows = 2 * set_rows
    smem = pl.BlockSpec(memory_space=pltpu.SMEM)
    vmem = pl.BlockSpec(memory_space=pltpu.VMEM)
    hbm = pl.BlockSpec(memory_space=pltpu.HBM)
    params = pltpu.CompilerParams(vmem_limit_bytes=VMEM_LIMIT)

    def in_hbm(*arrays):
        return [pltpu.with_memory_space_constraint(array, pltpu.HBM) for array in arrays]

    flips = list(range(2, strips))
    blocks = [0, 1] + flips
    filled = block_rows * len(blocks) + 2 * set_rows
    columns = round_up(filled, LANES)
    column = np.arange(columns)
    in_blocks = column < block_rows * len(blocks)
    block = np.minimum(column // block_rows, len(blocks) - 1)
    within = column % block_rows
    flip = np.where(in_blocks, np.asarray(blocks)[block], within // set_rows)
    kind = np.where(in_blocks, within // set_rows, np.where(column < filled, 2, 3))
    token = (within % set_rows) // 2
    whose, step = np.asarray([0, 0, 1, 1])[:, None], np.asarray([0, 1, 0, 1])[:, None]
    chosen = (within % 2 == 0) & (kind == np.where(flip == whose, step + 1, step))
    unused = np.zeros((2, columns))
    table = np.concatenate([chosen, flip[None], (token - lat_rows)[None], unused], axis=0).astype(np.int32)

    bf16 = functools.partial(jax.ShapeDtypeStruct, dtype=jnp.bfloat16)
    f32 = functools.partial(jax.ShapeDtypeStruct, dtype=jnp.float32)
    local_rows = query_rows + set_rows
    own, other, local, pair, mask = pl.pallas_call(
        functools.partial(pack_kernel, text_rows),
        out_shape=(
            bf16((block_rows, half)),
            bf16((block_rows, half)),
            bf16((local_rows, half)),
            bf16((block_rows + local_rows, half)),
            jax.ShapeDtypeStruct((5, columns), jnp.int32),
        ),
        in_specs=[hbm] * 4,
        out_specs=(vmem,) * 5,
        scratch_shapes=[
            pltpu.VMEM(table.shape, jnp.int32),
            pltpu.VMEM((strip_rows, 2, width), jnp.bfloat16),
            pltpu.VMEM((2, strip_rows, 2, width), jnp.bfloat16),
            pltpu.VMEM((2, lat_rows, width), jnp.bfloat16),
            pltpu.SemaphoreType.DMA((4,)),
        ],
        compiler_params=params,
    )(*in_hbm(jnp.asarray(table), stale_pairs.transpose(1, 0, 2), step_pairs.transpose(0, 2, 1, 3), queries))

    def to(rows, flip):
        return lax.ppermute(rows, "patch", [(i, i ^ flip) for i in range(strips)])

    held = {0: own}
    bit = strips // 2
    pair_rows = None
    while bit > 1:
        arrived = {bit: to(own, bit), bit + 1: to(other, bit + 1)}
        if pair_rows is None:
            pair_rows = to(pair, 1)
        for flip, rows in held.items():
            if flip > 1:
                arrived[flip + bit] = to(rows, bit)
        held.update(arrived)
        bit //= 2

    mine, back = pl.pallas_call(
        functools.partial(attention_kernel, (set_rows, query_rows)),
        out_shape=(bf16((query_rows, half)),) * 2,
        in_specs=[smem] + [vmem] * (4 + len(flips)),
        out_specs=(vmem, vmem),
        compiler_params=params,
    )(text_len, mask, own, local, pair_rows, *[held[flip] for flip in flips])
    returned = to(back, 1)

    model = out_weight.shape[1]
    total, gates, far_weight = pl.pallas_call(
        first_half_kernel,
        out_shape=(f32((lat_rows, model)), f32((2, model)), bf16((half, model))),
        in_specs=[vmem] + [hbm] * 4,
        out_specs=(vmem,) * 3,
        scratch_shapes=[
            pltpu.SMEM(t_index.shape, jnp.int32),
            pltpu.VMEM(gate_table.shape, jnp.bfloat16),
            pltpu.VMEM(hidden.shape, jnp.bfloat16),
            pltpu.VMEM((half, model), jnp.bfloat16),
            pltpu.SemaphoreType.DMA((5,)),
        ],
        compiler_params=params,
    )(mine, *in_hbm(t_index, gate_table, hidden, out_weight))
    keep, send = pl.pallas_call(
        second_half_kernel,
        out_shape=(f32((lat_rows // 2, model)), bf16((lat_rows // 2, model))),
        in_specs=[vmem] * 4,
        out_specs=(vmem, vmem),
        scratch_shapes=[pltpu.VMEM((lat_rows, model), jnp.float32)],
        compiler_params=params,
    )(returned, far_weight, gates, total)
    received = lax.ppermute(send, "head", [(0, 1), (1, 0)])
    return (keep + received.astype(jnp.float32)).astype(jnp.bfloat16)


def solution(mesh):
    return jax.shard_map(
        per_device,
        mesh=mesh,
        in_specs=(
            P(None, ("groups", "patch"), "head"),
            P(None, ("groups", "patch"), "head"),
            P(None, None, ("groups", "patch"), "head"),
            P(("groups", "patch"), "head"),
            P("head", None),
            P(),
            P("groups"),
            P("groups"),
        ),
        out_specs=P(("groups", "patch", "head"), None),
        check_vma=False,
    )
```

```python
import functools

import jax
import jax.numpy as jnp
import numpy as np
from jax import lax
from jax.experimental import pallas as pl
from jax.experimental.pallas import tpu as pltpu
from jax.sharding import PartitionSpec as P

HDIM = 128
LANES = 128
MASKED = -1e30
PAIR = 2
VMEM_LIMIT = 24 * 1024 * 1024


def round_up(value, step):
    return (value + step - 1) // step * step


def side_of(strip):
    return lax.rem(lax.div(strip, PAIR), 2)


def pack_kernel(text_rows, table_hbm, stale_hbm, step_hbm, query_hbm, own_ref, send_ref, other_ref, local_ref, pair_ref, mask_ref,
                table_ref, stale, step, query, sems):
    copies = [
        pltpu.make_async_copy(stale_hbm, stale, sems.at[0]),
        pltpu.make_async_copy(step_hbm, step, sems.at[1]),
        pltpu.make_async_copy(query_hbm, query, sems.at[2]),
        pltpu.make_async_copy(table_hbm, table_ref, sems.at[3]),
    ]
    for copy in copies:
        copy.start()
    strip = lax.axis_index("patch")
    side = side_of(strip)
    half = own_ref.shape[1]
    for copy in copies:
        copy.wait()
    early = table_ref[5:6, :]
    mask_ref[0:4, :] = table_ref[0:4, :]
    mask_ref[4:5, :] = jnp.where(early < 0, -1, (strip ^ table_ref[4:5, :]) * text_rows + early)

    def pick(ref, lead, which):
        lanes = pl.ds(pl.multiple_of(which * half, LANES), half)
        rows = ref[lead + (slice(None),) * (len(ref.shape) - len(lead) - 1) + (lanes,)]
        return rows.reshape(-1, half)

    for which, block_ref, rest_ref in ((side, own_ref, local_ref), (1 - side, other_ref, pair_ref)):
        block = jnp.concatenate([pick(stale, (), which), pick(step, (0,), which)], axis=0)
        rest = jnp.concatenate([pick(query, (), which), pick(step, (1,), which)], axis=0)
        block_ref[...] = block
        if block_ref is own_ref:
            send_ref[...] = block
        if rest_ref is pair_ref:
            rest = jnp.concatenate([block, rest], axis=0)
        spare = rest_ref.shape[0] - rest.shape[0]
        rest_ref[...] = jnp.concatenate([rest, jnp.zeros((spare, half), rest.dtype)], axis=0) if spare else rest


def blocks_of(ref):
    return [slice(i, i + HDIM) for i in range(0, ref.shape[-1], HDIM)]


def queries_of(local_ref, pair_ref, query_rows, lanes):
    block_rows = pair_ref.shape[0] - local_ref.shape[0]
    return jnp.concatenate(
        [local_ref[:query_rows, lanes], pair_ref[block_rows : block_rows + query_rows, lanes]], axis=0
    )


def scored(queries, parts, bias):
    filled = sum(part.shape[0] for part in parts)
    if filled < bias.shape[1]:
        parts = parts + [jnp.zeros((bias.shape[1] - filled, HDIM), jnp.bfloat16)]
    rows = jnp.concatenate(parts, axis=0)
    scores = lax.dot_general(queries, rows, (((1,), (1,)), ((), ())), preferred_element_type=jnp.float32)
    return rows, scores * (1.0 / HDIM**0.5) + bias


def weigh(expo, rows):
    return jnp.dot(pltpu.roll(expo, 1, 1).astype(jnp.bfloat16), rows, preferred_element_type=jnp.float32)


def spread(bias, count):
    return jnp.concatenate(
        [jnp.broadcast_to(bias[c : c + 1, :], (count, bias.shape[1])) for c in range(bias.shape[0])], axis=0
    )


def early_attention_kernel(sizes, text_ref, mask_ref, own_ref, local_ref, pair_ref, *refs):
    query_rows, columns = sizes
    others, (mixed_ref, top_ref, norm_ref, bias_ref) = refs[:-4], refs[-4:]
    block_rows = own_ref.shape[0]
    live = mask_ref[4:5, :] < text_ref[0]
    bias = jnp.where((mask_ref[0:4, :] > 0) & live, 0.0, MASKED)
    bias_ref[...] = bias[:, columns:]
    bias = spread(bias[:, :columns], query_rows // 2)
    work = []
    for lanes in blocks_of(own_ref):
        parts = [own_ref[:, lanes], pair_ref[:block_rows, lanes]] + [ref[:, lanes] for ref in others]
        parts += [local_ref[query_rows:, lanes], pair_ref[block_rows + query_rows :, lanes]]
        work.append(scored(queries_of(local_ref, pair_ref, query_rows, lanes), parts, bias))
    tops = [jnp.max(scores, axis=1, keepdims=True) for _, scores in work]
    expos = [jnp.exp(scores - top) for (_, scores), top in zip(work, tops)]
    for lanes, (rows, _), top, expo in zip(blocks_of(own_ref), work, tops, expos):
        shape = (2 * query_rows, HDIM)
        mixed_ref[:, lanes] = weigh(expo, rows)
        top_ref[:, lanes] = jnp.broadcast_to(top, shape)
        norm_ref[:, lanes] = jnp.broadcast_to(jnp.sum(expo, axis=1, keepdims=True), shape)


def late_attention_kernel(query_rows, bias_ref, local_ref, pair_ref, mixed_ref, top_ref, norm_ref, *refs):
    others, (mine_ref, back_ref) = refs[:-2], refs[-2:]
    bias = spread(bias_ref[...], query_rows // 2)
    lane_blocks = blocks_of(local_ref)
    work = [
        scored(queries_of(local_ref, pair_ref, query_rows, lanes), [ref[:, lanes] for ref in others], bias)
        for lanes in lane_blocks
    ]
    tops = [
        jnp.maximum(jnp.max(scores, axis=1, keepdims=True), top_ref[:, lanes])
        for lanes, (_, scores) in zip(lane_blocks, work)
    ]
    expos = [jnp.exp(scores - top[:, :1]) for (_, scores), top in zip(work, tops)]
    for lanes, (rows, _), top, expo in zip(lane_blocks, work, tops, expos):
        shrink = jnp.exp(top_ref[:, lanes] - top)
        norm = norm_ref[:, lanes] * shrink + jnp.sum(expo, axis=1, keepdims=True)
        mixed = ((mixed_ref[:, lanes] * shrink + weigh(expo, rows)) / norm).astype(jnp.bfloat16)
        mine_ref[:, lanes] = mixed[:query_rows]
        back_ref[:, lanes] = mixed[query_rows:]


def gated(attended, weight, gates):
    strip = attended.shape[0] // 2
    projected = jnp.dot(attended, weight, preferred_element_type=jnp.float32)
    return gates[0:1, :] * projected[:strip] + gates[1:2, :] * projected[strip:]


def first_half_kernel(attended_ref, plan_hbm, table_hbm, hidden_hbm, weight_hbm, sum_ref, gates_ref, far_ref,
                      plan_ref, table_ref, hidden_ref, near, sems):
    depth = attended_ref.shape[1]
    width = hidden_ref.shape[1]
    side = side_of(lax.axis_index("patch"))
    rows = pl.ds(pl.multiple_of(side * depth, depth), depth)
    far_rows = pl.ds(pl.multiple_of((1 - side) * depth, depth), depth)
    near_copy = pltpu.make_async_copy(weight_hbm.at[rows, :], near, sems.at[0])
    far_copy = pltpu.make_async_copy(weight_hbm.at[far_rows, :], far_ref, sems.at[1])
    small = [
        pltpu.make_async_copy(plan_hbm, plan_ref, sems.at[2]),
        pltpu.make_async_copy(table_hbm, table_ref, sems.at[3]),
        pltpu.make_async_copy(hidden_hbm, hidden_ref, sems.at[4]),
    ]
    for copy in small + [near_copy, far_copy]:
        copy.start()
    for copy in small:
        copy.wait()
    table = table_ref[...].astype(jnp.float32)
    entry = lax.broadcasted_iota(jnp.int32, table.shape, 0)
    for step in range(2):
        row = jnp.sum(jnp.where(entry == plan_ref[step], table, 0.0), axis=0, keepdims=True)
        gates_ref[step : step + 1, :] = row
    near_copy.wait()
    sum_ref[...] = gated(attended_ref[...], near[...], gates_ref[...])
    lanes = pl.ds(pl.multiple_of(lax.axis_index("head") * width, LANES), width)
    sum_ref[:, lanes] += hidden_ref[...].astype(jnp.float32)
    far_copy.wait()


def second_half_kernel(attended_ref, weight_ref, gates_ref, sum_ref, keep_ref, send_ref, total):
    half = keep_ref.shape[0]
    total[...] = sum_ref[...] + gated(attended_ref[...], weight_ref[...], gates_ref[...])
    core = lax.axis_index("head")
    keep_ref[...] = total[pl.ds(pl.multiple_of(core * half, half), half), :]
    send_ref[...] = total[pl.ds(pl.multiple_of((1 - core) * half, half), half), :].astype(jnp.bfloat16)


def per_device(queries, stale_pairs, step_pairs, hidden, out_weight, gate_table, t_index, text_len):
    strips = lax.axis_size("patch")
    strip_rows = stale_pairs.shape[1]
    lat_rows = queries.shape[1]
    text_rows = strip_rows - lat_rows
    width = queries.shape[2]
    half = width // 2
    set_rows = 2 * strip_rows
    query_rows = 2 * lat_rows
    block_rows = 2 * set_rows
    smem = pl.BlockSpec(memory_space=pltpu.SMEM)
    vmem = pl.BlockSpec(memory_space=pltpu.VMEM)
    hbm = pl.BlockSpec(memory_space=pltpu.HBM)
    params = pltpu.CompilerParams(vmem_limit_bytes=VMEM_LIMIT)

    def in_hbm(*arrays):
        return [pltpu.with_memory_space_constraint(array, pltpu.HBM) for array in arrays]

    late = [flip for flip in range(4, strips) if flip % 2]
    early = [0, PAIR] + [flip for flip in range(1, strips) if flip != PAIR and flip not in late]
    pieces = [[(flip, kind) for flip in early for kind in (0, 1)] + [(0, 2), (PAIR, 2)]]
    pieces.append([(flip, kind) for flip in late for kind in (0, 1)])
    whose, step = np.asarray([0, 0, PAIR, PAIR])[:, None], np.asarray([0, 1, 0, 1])[:, None]
    tables = []
    for part in pieces:
        column = np.arange(round_up(set_rows * len(part), LANES))
        within = column % set_rows
        filled = column < set_rows * len(part)
        flip, kind = np.asarray(part)[np.minimum(column // set_rows, len(part) - 1)].T
        chosen = filled & (within % 2 == 0) & (kind == np.where(flip == whose, step + 1, step))
        tables.append(np.concatenate([chosen, flip[None], (within // 2 - lat_rows)[None]], axis=0))
    early_columns = tables[0].shape[1]
    table = np.concatenate(tables, axis=1).astype(np.int32)
    columns = table.shape[1]

    bf16 = functools.partial(jax.ShapeDtypeStruct, dtype=jnp.bfloat16)
    f32 = functools.partial(jax.ShapeDtypeStruct, dtype=jnp.float32)
    local_rows = query_rows + set_rows
    own, sent, other, local, pair, mask = pl.pallas_call(
        functools.partial(pack_kernel, text_rows),
        out_shape=(
            bf16((block_rows, half)),
            bf16((block_rows, half)),
            bf16((block_rows, half)),
            bf16((local_rows, half)),
            bf16((block_rows + local_rows, half)),
            jax.ShapeDtypeStruct((5, columns), jnp.int32),
        ),
        in_specs=[hbm] * 4,
        out_specs=(vmem,) * 6,
        scratch_shapes=[
            pltpu.VMEM(table.shape, jnp.int32),
            pltpu.VMEM((strip_rows, 2, width), jnp.bfloat16),
            pltpu.VMEM((2, strip_rows, 2, width), jnp.bfloat16),
            pltpu.VMEM((2, lat_rows, width), jnp.bfloat16),
            pltpu.SemaphoreType.DMA((4,)),
        ],
        compiler_params=params,
    )(*in_hbm(jnp.asarray(table), stale_pairs.transpose(1, 0, 2), step_pairs.transpose(0, 2, 1, 3), queries))

    def to(rows, flip):
        return lax.ppermute(rows, "patch", [(i, i ^ flip) for i in range(strips)])

    held = {}
    pair_rows = None
    bit = strips // 2
    while bit:
        if bit != PAIR:
            arrived = {bit ^ PAIR: to(other, bit ^ PAIR), bit: to(sent, bit)}
            if pair_rows is None:
                pair_rows = to(pair, PAIR)
            for flip, rows in held.items():
                arrived[flip ^ bit] = to(rows, bit)
            held.update(arrived)
        bit //= 2

    *first, late_bias = pl.pallas_call(
        functools.partial(early_attention_kernel, (query_rows, early_columns)),
        out_shape=(f32((2 * query_rows, half)),) * 3 + (f32((4, columns - early_columns)),),
        in_specs=[smem] + [vmem] * (2 + len(early)),
        out_specs=(vmem,) * 4,
        compiler_params=params,
    )(text_len, mask, own, local, pair_rows, *[held[flip] for flip in early[2:]])
    mine, back = pl.pallas_call(
        functools.partial(late_attention_kernel, query_rows),
        out_shape=(bf16((query_rows, half)),) * 2,
        in_specs=[vmem] * (6 + len(late)),
        out_specs=(vmem, vmem),
        compiler_params=params,
    )(late_bias, local, pair_rows, *first, *[held[flip] for flip in late])
    returned = to(back, PAIR)

    model = out_weight.shape[1]
    total, gates, far_weight = pl.pallas_call(
        first_half_kernel,
        out_shape=(f32((lat_rows, model)), f32((2, model)), bf16((half, model))),
        in_specs=[vmem] + [hbm] * 4,
        out_specs=(vmem,) * 3,
        scratch_shapes=[
            pltpu.SMEM(t_index.shape, jnp.int32),
            pltpu.VMEM(gate_table.shape, jnp.bfloat16),
            pltpu.VMEM(hidden.shape, jnp.bfloat16),
            pltpu.VMEM((half, model), jnp.bfloat16),
            pltpu.SemaphoreType.DMA((5,)),
        ],
        compiler_params=params,
    )(mine, *in_hbm(t_index, gate_table, hidden, out_weight))
    keep, send = pl.pallas_call(
        second_half_kernel,
        out_shape=(f32((lat_rows // 2, model)), bf16((lat_rows // 2, model))),
        in_specs=[vmem] * 4,
        out_specs=(vmem, vmem),
        scratch_shapes=[pltpu.VMEM((lat_rows, model), jnp.float32)],
        compiler_params=params,
    )(returned, far_weight, gates, total)
    received = lax.ppermute(send, "head", [(0, 1), (1, 0)])
    return (keep + received.astype(jnp.float32)).astype(jnp.bfloat16)


def solution(mesh):
    return jax.shard_map(
        per_device,
        mesh=mesh,
        in_specs=(
            P(None, ("groups", "patch"), "head"),
            P(None, ("groups", "patch"), "head"),
            P(None, None, ("groups", "patch"), "head"),
            P(("groups", "patch"), "head"),
            P("head", None),
            P(),
            P("groups"),
            P("groups"),
        ),
        out_specs=P(("groups", "patch", "head"), None),
        check_vma=False,
    )
```

```python
import functools

import jax
import jax.numpy as jnp
import numpy as np
from jax import lax
from jax.experimental import pallas as pl
from jax.experimental.pallas import tpu as pltpu
from jax.sharding import PartitionSpec as P

HDIM = 128
LANES = 128
MASKED = -1e30
VMEM_LIMIT = 24 * 1024 * 1024
TERMS, TERM_LANES = 3, 32
CHUNKS = 6


def round_up(value, step):
    return (value + step - 1) // step * step


def pack_kernel(text_rows, table_hbm, stale_hbm, step_hbm, query_hbm, block_ref, local_ref, query_ref, mask_ref,
                table_ref, stale, step, query, sems):
    copies = [
        pltpu.make_async_copy(stale_hbm, stale, sems.at[0]),
        pltpu.make_async_copy(step_hbm, step, sems.at[1]),
        pltpu.make_async_copy(query_hbm, query, sems.at[2]),
        pltpu.make_async_copy(table_hbm, table_ref, sems.at[3]),
    ]
    for copy in copies:
        copy.start()
    for copy in copies:
        copy.wait()
    strip = lax.axis_index("patch")
    classes = mask_ref.shape[0] - 1
    early = table_ref[classes + 1 : classes + 2, :]
    mask_ref[:classes, :] = table_ref[:classes, :]
    mask_ref[classes:, :] = jnp.where(early < 0, -1, (strip ^ table_ref[classes : classes + 1, :]) * text_rows + early)
    width = block_ref.shape[1]
    block_ref[...] = jnp.concatenate([stale[...].reshape(-1, width), step[0].reshape(-1, width)], axis=0)
    query_ref[...] = query[...].reshape(-1, width)
    local_ref[...] = jnp.concatenate([query[...].reshape(-1, width), step[1].reshape(-1, width)], axis=0)


def blocks_of(ref):
    return [slice(i, i + HDIM) for i in range(0, ref.shape[-1], HDIM)]


def attention(query_rows, bias_ref, own_ref, local_ref, query_ref, others, first_class):
    columns = bias_ref.shape[1]
    bias = jnp.concatenate(
        [jnp.broadcast_to(bias_ref[first_class + c : first_class + c + 1, :], (query_rows // 2, columns)) for c in range(2)],
        axis=0,
    )
    lane_blocks = blocks_of(own_ref)
    rows, scores = [], []
    for lanes in lane_blocks:
        parts = [own_ref[:, lanes]] + [ref[:, lanes] for ref in others] + [local_ref[query_rows:, lanes]]
        filled = sum(part.shape[0] for part in parts)
        if filled < columns:
            parts.append(jnp.zeros((columns - filled, HDIM), jnp.bfloat16))
        rows.append(jnp.concatenate(parts, axis=0))
        scores.append(
            lax.dot_general(
                query_ref[:query_rows, lanes], rows[-1], (((1,), (1,)), ((), ())), preferred_element_type=jnp.float32
            )
            * (1.0 / HDIM**0.5)
            + bias
        )
    tops = [jnp.max(score, axis=1, keepdims=True) for score in scores]
    expos = [jnp.exp(score - top) for score, top in zip(scores, tops)]
    norms = [jnp.sum(expo, axis=1, keepdims=True) for expo in expos]
    lane = lax.broadcasted_iota(jnp.int32, (query_rows, LANES), 1)
    logs = jnp.zeros((query_rows, LANES), jnp.float32)
    mixed = []
    for head, (expo, norm, top, row) in enumerate(zip(expos, norms, tops, rows)):
        weights = pltpu.roll(expo / norm, 1, 1).astype(jnp.bfloat16)
        mixed.append(jnp.dot(weights, row, preferred_element_type=jnp.float32))
        logs = jnp.where(lane == head, top + jnp.log(norm), logs)
    return mixed, logs


def own_kernel(query_rows, bias_ref, own_ref, local_ref, *refs):
    others, (mixed_ref, log_ref) = refs[:-2], refs[-2:]
    mixed, logs = attention(query_rows, bias_ref, own_ref, local_ref, local_ref, others, 0)
    for lanes, rows in zip(blocks_of(own_ref), mixed):
        mixed_ref[:, lanes] = rows
    log_ref[...] = logs


def partner_kernel(query_rows, bias_ref, own_ref, local_ref, query_ref, *refs):
    others, partner_ref = refs[:-1], refs[-1]
    mixed, rest = attention(query_rows, bias_ref, own_ref, local_ref, query_ref, others, 2)
    for lanes, rows in zip(blocks_of(own_ref), mixed):
        partner_ref[:, lanes] = rows.astype(jnp.bfloat16)
    coded = jnp.zeros_like(rest)
    for term in range(TERMS):
        part = rest.astype(jnp.bfloat16).astype(jnp.float32)
        coded = coded + (pltpu.roll(part, term * TERM_LANES, 1) if term else part)
        rest = rest - part
    partner_ref[:, own_ref.shape[1] :] = coded.astype(jnp.bfloat16)


def decoded(packed_ref, width):
    coded = packed_ref[:, width:].astype(jnp.float32)
    logs = pltpu.roll(coded, LANES - 2 * TERM_LANES, 1) + pltpu.roll(coded, LANES - TERM_LANES, 1) + coded
    return packed_ref[:, :width].astype(jnp.float32), logs


def joined(one, two, lane_blocks):
    (mixed, logs), (other_mixed, other_logs) = one, two
    parts = []
    for head, lanes in enumerate(lane_blocks):
        log, other_log = logs[:, head : head + 1], other_logs[:, head : head + 1]
        top = jnp.maximum(log, other_log)
        share, other_share = jnp.exp(log - top), jnp.exp(other_log - top)
        whole = share + other_share
        parts.append(mixed[:, lanes] * (share / whole) + other_mixed[:, lanes] * (other_share / whole))
    return jnp.concatenate(parts, axis=1).astype(jnp.bfloat16)


def fetch_kernel(text_ref, mask_ref, plan_hbm, table_hbm, hidden_hbm, weight_hbm, bias_ref, sum_ref, gates_ref, weight_ref,
                 plan_ref, table_ref, hidden_ref, sems):
    small = [
        pltpu.make_async_copy(plan_hbm, plan_ref, sems.at[0]),
        pltpu.make_async_copy(table_hbm, table_ref, sems.at[1]),
        pltpu.make_async_copy(hidden_hbm, hidden_ref, sems.at[2]),
    ]
    depth = weight_ref.shape[0] // CHUNKS
    large = [
        pltpu.make_async_copy(
            weight_hbm.at[pl.ds(chunk * depth, depth), :], weight_ref.at[pl.ds(chunk * depth, depth), :], sems.at[3 + chunk]
        )
        for chunk in range(CHUNKS)
    ]
    for copy in small + large:
        copy.start()
    classes = bias_ref.shape[0]
    live = mask_ref[classes:, :] < text_ref[0]
    bias_ref[...] = jnp.where((mask_ref[:classes, :] > 0) & live, 0.0, MASKED)
    for copy in small:
        copy.wait()
    table = table_ref[...].astype(jnp.float32)
    entry = lax.broadcasted_iota(jnp.int32, table.shape, 0)
    for step in range(2):
        row = jnp.sum(jnp.where(entry == plan_ref[step], table, 0.0), axis=0, keepdims=True)
        gates_ref[step : step + 1, :] = row
    width = hidden_ref.shape[1]
    lanes = pl.ds(pl.multiple_of(lax.axis_index("head") * width, LANES), width)
    sum_ref[...] = jnp.zeros_like(sum_ref)
    sum_ref[:, lanes] = hidden_ref[...].astype(jnp.float32)
    for copy in large:
        copy.wait()


def project_kernel(mixed_ref, log_ref, partner_ref, weight_ref, gates_ref, sum_ref, keep_ref, send_ref):
    strip = sum_ref.shape[0]
    half = keep_ref.shape[0]
    attended = joined((mixed_ref[...], log_ref[...]), decoded(partner_ref, mixed_ref.shape[1]), blocks_of(mixed_ref))
    projected = jnp.dot(attended, weight_ref[...], preferred_element_type=jnp.float32)
    total = sum_ref[...] + gates_ref[0:1, :] * projected[:strip] + gates_ref[1:2, :] * projected[strip:]
    first = lax.axis_index("head") == 0
    keep_ref[...] = jnp.where(first, total[:half], total[half:])
    send_ref[...] = jnp.where(first, total[half:], total[:half]).astype(jnp.bfloat16)


def per_device(queries, stale_pairs, step_pairs, hidden, out_weight, gate_table, t_index, text_len):
    strips = lax.axis_size("patch")
    strip_rows = stale_pairs.shape[1]
    lat_rows = queries.shape[1]
    text_rows = strip_rows - lat_rows
    width = queries.shape[2]
    model = out_weight.shape[1]
    set_rows = 2 * strip_rows
    query_rows = 2 * lat_rows
    block_rows = 2 * set_rows
    smem = pl.BlockSpec(memory_space=pltpu.SMEM)
    vmem = pl.BlockSpec(memory_space=pltpu.VMEM)
    hbm = pl.BlockSpec(memory_space=pltpu.HBM)
    params = pltpu.CompilerParams(vmem_limit_bytes=VMEM_LIMIT)

    def in_hbm(*arrays):
        return [pltpu.with_memory_space_constraint(array, pltpu.HBM) for array in arrays]

    across = strips // 2
    neighbours = sorted(range(1, across), key=lambda flip: (-bin(flip).count("1"), flip))
    pieces = [(flip, kind) for flip in [0] + neighbours for kind in (0, 1)] + [(0, 2)]
    whose, step = np.asarray([0, 0, across, across])[:, None], np.asarray([0, 1, 0, 1])[:, None]
    columns = round_up(set_rows * len(pieces), LANES)
    column = np.arange(columns)
    within = column % set_rows
    flip, kind = np.asarray(pieces)[np.minimum(column // set_rows, len(pieces) - 1)].T
    is_key = (column < set_rows * len(pieces)) & (within % 2 == 0)
    chosen = is_key & (kind == np.where(flip == whose, step + 1, step))
    table = np.concatenate([chosen, flip[None], (within // 2 - lat_rows)[None]], axis=0).astype(np.int32)

    bf16 = functools.partial(jax.ShapeDtypeStruct, dtype=jnp.bfloat16)
    f32 = functools.partial(jax.ShapeDtypeStruct, dtype=jnp.float32)
    block, local, query, mask = pl.pallas_call(
        functools.partial(pack_kernel, text_rows),
        out_shape=(
            bf16((block_rows, width)),
            bf16((query_rows + set_rows, width)),
            bf16((query_rows, width)),
            jax.ShapeDtypeStruct((len(whose) + 1, columns), jnp.int32),
        ),
        in_specs=[hbm] * 4,
        out_specs=(vmem,) * 4,
        scratch_shapes=[
            pltpu.VMEM(table.shape, jnp.int32),
            pltpu.VMEM((strip_rows, 2, width), jnp.bfloat16),
            pltpu.VMEM((2, strip_rows, 2, width), jnp.bfloat16),
            pltpu.VMEM((2, lat_rows, width), jnp.bfloat16),
            pltpu.SemaphoreType.DMA((4,)),
        ],
        compiler_params=params,
    )(*in_hbm(jnp.asarray(table), stale_pairs.transpose(1, 0, 2), step_pairs.transpose(0, 2, 1, 3), queries))

    def to(rows, flip):
        return lax.ppermute(rows, "patch", [(i, i ^ flip) for i in range(strips)])

    partner_query = to(query, across)
    others = [to(block, flip) for flip in neighbours]
    bias, total, gates, weight = pl.pallas_call(
        fetch_kernel,
        out_shape=(f32((len(whose), columns)), f32((lat_rows, model)), f32((2, model)), bf16(out_weight.shape)),
        in_specs=[smem, vmem] + [hbm] * 4,
        out_specs=(vmem,) * 4,
        scratch_shapes=[
            pltpu.SMEM(t_index.shape, jnp.int32),
            pltpu.VMEM(gate_table.shape, jnp.bfloat16),
            pltpu.VMEM(hidden.shape, jnp.bfloat16),
            pltpu.SemaphoreType.DMA((3 + CHUNKS,)),
        ],
        compiler_params=params,
    )(text_len, mask, *in_hbm(t_index, gate_table, hidden, out_weight))
    partial_rows = pl.pallas_call(
        functools.partial(partner_kernel, query_rows),
        out_shape=bf16((query_rows, width + LANES)),
        in_specs=[vmem] * (4 + len(others)),
        out_specs=vmem,
        compiler_params=params,
    )(bias, block, local, partner_query, *others)
    mixed, logs = pl.pallas_call(
        functools.partial(own_kernel, query_rows),
        out_shape=(f32((query_rows, width)), f32((query_rows, LANES))),
        in_specs=[vmem] * (3 + len(others)),
        out_specs=(vmem,) * 2,
        compiler_params=params,
    )(bias, block, local, *others)
    partner_rows = to(partial_rows, across)

    keep, send = pl.pallas_call(
        project_kernel,
        out_shape=(f32((lat_rows // 2, model)), bf16((lat_rows // 2, model))),
        in_specs=[vmem] * 6,
        out_specs=(vmem, vmem),
        compiler_params=params,
    )(mixed, logs, partner_rows, weight, gates, total)
    received = lax.ppermute(send, "head", [(0, 1), (1, 0)])
    return (keep + received.astype(jnp.float32)).astype(jnp.bfloat16)


def solution(mesh):
    return jax.shard_map(
        per_device,
        mesh=mesh,
        in_specs=(
            P(None, ("groups", "patch"), "head"),
            P(None, ("groups", "patch"), "head"),
            P(None, None, ("groups", "patch"), "head"),
            P(("groups", "patch"), "head"),
            P("head", None),
            P(),
            P("groups"),
            P("groups"),
        ),
        out_specs=P(("groups", "patch", "head"), None),
        check_vma=False,
    )
```

```python
import functools

import jax
import jax.numpy as jnp
import numpy as np
from jax import lax
from jax.experimental import pallas as pl
from jax.experimental.pallas import tpu as pltpu
from jax.sharding import PartitionSpec as P

HDIM = 128
LANES = 128
MASKED = -1e30
VMEM_LIMIT = 24 * 1024 * 1024
TERMS, TERM_LANES = 3, 32
CHUNKS = 6


def round_up(value, step):
    return (value + step - 1) // step * step


def pack_kernel(text_rows, table_hbm, stale_hbm, step_hbm, query_hbm, block_ref, local_ref, query_ref, mask_ref,
                table_ref, stale, step, query, sems):
    copies = [
        pltpu.make_async_copy(stale_hbm, stale, sems.at[0]),
        pltpu.make_async_copy(step_hbm, step, sems.at[1]),
        pltpu.make_async_copy(query_hbm, query, sems.at[2]),
        pltpu.make_async_copy(table_hbm, table_ref, sems.at[3]),
    ]
    for copy in copies:
        copy.start()
    for copy in copies:
        copy.wait()
    strip = lax.axis_index("patch")
    classes = mask_ref.shape[0] - 1
    early = table_ref[classes + 1 : classes + 2, :]
    mask_ref[:classes, :] = table_ref[:classes, :]
    mask_ref[classes:, :] = jnp.where(early < 0, -1, (strip ^ table_ref[classes : classes + 1, :]) * text_rows + early)
    width = block_ref.shape[1]
    block_ref[...] = jnp.concatenate([stale[...].reshape(-1, width), step[0].reshape(-1, width)], axis=0)
    query_ref[...] = query[...].reshape(-1, width)
    local_ref[...] = jnp.concatenate([query[...].reshape(-1, width), step[1].reshape(-1, width)], axis=0)


def blocks_of(ref):
    return [slice(i, i + HDIM) for i in range(0, ref.shape[-1], HDIM)]


def attention(query_rows, bias_ref, own_ref, local_ref, query_ref, others, first_class):
    columns = bias_ref.shape[1]
    bias = jnp.concatenate(
        [jnp.broadcast_to(bias_ref[first_class + c : first_class + c + 1, :], (query_rows // 2, columns)) for c in range(2)],
        axis=0,
    )
    lane_blocks = blocks_of(own_ref)
    rows, scores = [], []
    for lanes in lane_blocks:
        parts = [own_ref[:, lanes]] + [ref[:, lanes] for ref in others] + [local_ref[query_rows:, lanes]]
        filled = sum(part.shape[0] for part in parts)
        if filled < columns:
            parts.append(jnp.zeros((columns - filled, HDIM), jnp.bfloat16))
        rows.append(jnp.concatenate(parts, axis=0))
        scores.append(
            lax.dot_general(
                query_ref[:query_rows, lanes], rows[-1], (((1,), (1,)), ((), ())), preferred_element_type=jnp.float32
            )
            * (1.0 / HDIM**0.5)
            + bias
        )
    tops = [jnp.max(score, axis=1, keepdims=True) for score in scores]
    expos = [jnp.exp(score - top) for score, top in zip(scores, tops)]
    norms = [jnp.sum(expo, axis=1, keepdims=True) for expo in expos]
    sums = [
        jnp.dot(pltpu.roll(expo, 1, 1).astype(jnp.bfloat16), row, preferred_element_type=jnp.float32)
        for expo, row in zip(expos, rows)
    ]
    mixed = [whole * (1.0 / norm) for whole, norm in zip(sums, norms)]
    lane = lax.broadcasted_iota(jnp.int32, (query_rows, LANES), 1)
    all_norms, all_tops = jnp.ones((query_rows, LANES), jnp.float32), jnp.zeros((query_rows, LANES), jnp.float32)
    for head, (norm, top) in enumerate(zip(norms, tops)):
        all_norms = jnp.where(lane == head, norm, all_norms)
        all_tops = jnp.where(lane == head, top, all_tops)
    logs = all_tops + jnp.log(all_norms)
    return mixed, logs


def own_kernel(query_rows, bias_ref, own_ref, local_ref, *refs):
    others, (mixed_ref, log_ref) = refs[:-2], refs[-2:]
    mixed, logs = attention(query_rows, bias_ref, own_ref, local_ref, local_ref, others, 0)
    for lanes, rows in zip(blocks_of(own_ref), mixed):
        mixed_ref[:, lanes] = rows
    log_ref[...] = logs


def partner_kernel(query_rows, bias_ref, own_ref, local_ref, query_ref, *refs):
    others, partner_ref = refs[:-1], refs[-1]
    mixed, rest = attention(query_rows, bias_ref, own_ref, local_ref, query_ref, others, 2)
    for lanes, rows in zip(blocks_of(own_ref), mixed):
        partner_ref[:, lanes] = rows.astype(jnp.bfloat16)
    coded = jnp.zeros_like(rest)
    for term in range(TERMS):
        part = rest.astype(jnp.bfloat16).astype(jnp.float32)
        coded = coded + (pltpu.roll(part, term * TERM_LANES, 1) if term else part)
        rest = rest - part
    partner_ref[:, own_ref.shape[1] :] = coded.astype(jnp.bfloat16)


def decoded(packed_ref, width):
    coded = packed_ref[:, width:].astype(jnp.float32)
    logs = pltpu.roll(coded, LANES - 2 * TERM_LANES, 1) + pltpu.roll(coded, LANES - TERM_LANES, 1) + coded
    return packed_ref[:, :width].astype(jnp.float32), logs


def joined(one, two, lane_blocks):
    (mixed, logs), (other_mixed, other_logs) = one, two
    parts = []
    for head, lanes in enumerate(lane_blocks):
        log, other_log = logs[:, head : head + 1], other_logs[:, head : head + 1]
        top = jnp.maximum(log, other_log)
        share, other_share = jnp.exp(log - top), jnp.exp(other_log - top)
        whole = share + other_share
        parts.append(mixed[:, lanes] * (share / whole) + other_mixed[:, lanes] * (other_share / whole))
    return jnp.concatenate(parts, axis=1).astype(jnp.bfloat16)


def fetch_kernel(text_ref, mask_ref, plan_hbm, table_hbm, hidden_hbm, weight_hbm, bias_ref, sum_ref, gates_ref, weight_ref,
                 plan_ref, table_ref, hidden_ref, sems):
    small = [
        pltpu.make_async_copy(plan_hbm, plan_ref, sems.at[0]),
        pltpu.make_async_copy(table_hbm, table_ref, sems.at[1]),
        pltpu.make_async_copy(hidden_hbm, hidden_ref, sems.at[2]),
    ]
    depth = weight_ref.shape[0] // CHUNKS
    large = [
        pltpu.make_async_copy(
            weight_hbm.at[pl.ds(chunk * depth, depth), :], weight_ref.at[pl.ds(chunk * depth, depth), :], sems.at[3 + chunk]
        )
        for chunk in range(CHUNKS)
    ]
    for copy in small + large:
        copy.start()
    classes = bias_ref.shape[0]
    live = mask_ref[classes:, :] < text_ref[0]
    bias_ref[...] = jnp.where((mask_ref[:classes, :] > 0) & live, 0.0, MASKED)
    for copy in small:
        copy.wait()
    table = table_ref[...].astype(jnp.float32)
    entry = lax.broadcasted_iota(jnp.int32, table.shape, 0)
    for step in range(2):
        row = jnp.sum(jnp.where(entry == plan_ref[step], table, 0.0), axis=0, keepdims=True)
        gates_ref[step : step + 1, :] = row
    width = hidden_ref.shape[1]
    lanes = pl.ds(pl.multiple_of(lax.axis_index("head") * width, LANES), width)
    sum_ref[...] = jnp.zeros_like(sum_ref)
    sum_ref[:, lanes] = hidden_ref[...].astype(jnp.float32)
    for copy in large:
        copy.wait()


def project_kernel(mixed_ref, log_ref, partner_ref, weight_ref, gates_ref, sum_ref, keep_ref, send_ref):
    strip = sum_ref.shape[0]
    half = keep_ref.shape[0]
    attended = joined((mixed_ref[...], log_ref[...]), decoded(partner_ref, mixed_ref.shape[1]), blocks_of(mixed_ref))
    projected = jnp.dot(attended, weight_ref[...], preferred_element_type=jnp.float32)
    total = sum_ref[...] + gates_ref[0:1, :] * projected[:strip] + gates_ref[1:2, :] * projected[strip:]
    first = lax.axis_index("head") == 0
    keep_ref[...] = jnp.where(first, total[:half], total[half:])
    send_ref[...] = jnp.where(first, total[half:], total[:half]).astype(jnp.bfloat16)


def per_device(queries, stale_pairs, step_pairs, hidden, out_weight, gate_table, t_index, text_len):
    strips = lax.axis_size("patch")
    strip_rows = stale_pairs.shape[1]
    lat_rows = queries.shape[1]
    text_rows = strip_rows - lat_rows
    width = queries.shape[2]
    model = out_weight.shape[1]
    set_rows = 2 * strip_rows
    query_rows = 2 * lat_rows
    block_rows = 2 * set_rows
    smem = pl.BlockSpec(memory_space=pltpu.SMEM)
    vmem = pl.BlockSpec(memory_space=pltpu.VMEM)
    hbm = pl.BlockSpec(memory_space=pltpu.HBM)
    params = pltpu.CompilerParams(vmem_limit_bytes=VMEM_LIMIT)

    def in_hbm(*arrays):
        return [pltpu.with_memory_space_constraint(array, pltpu.HBM) for array in arrays]

    across = strips // 2
    neighbours = sorted(range(1, across), key=lambda flip: (-bin(flip).count("1"), flip))
    pieces = [(flip, kind) for flip in [0] + neighbours for kind in (0, 1)] + [(0, 2)]
    whose, step = np.asarray([0, 0, across, across])[:, None], np.asarray([0, 1, 0, 1])[:, None]
    columns = round_up(set_rows * len(pieces), LANES)
    column = np.arange(columns)
    within = column % set_rows
    flip, kind = np.asarray(pieces)[np.minimum(column // set_rows, len(pieces) - 1)].T
    is_key = (column < set_rows * len(pieces)) & (within % 2 == 0)
    chosen = is_key & (kind == np.where(flip == whose, step + 1, step))
    table = np.concatenate([chosen, flip[None], (within // 2 - lat_rows)[None]], axis=0).astype(np.int32)

    bf16 = functools.partial(jax.ShapeDtypeStruct, dtype=jnp.bfloat16)
    f32 = functools.partial(jax.ShapeDtypeStruct, dtype=jnp.float32)
    block, local, query, mask = pl.pallas_call(
        functools.partial(pack_kernel, text_rows),
        out_shape=(
            bf16((block_rows, width)),
            bf16((query_rows + set_rows, width)),
            bf16((query_rows, width)),
            jax.ShapeDtypeStruct((len(whose) + 1, columns), jnp.int32),
        ),
        in_specs=[hbm] * 4,
        out_specs=(vmem,) * 4,
        scratch_shapes=[
            pltpu.VMEM(table.shape, jnp.int32),
            pltpu.VMEM((strip_rows, 2, width), jnp.bfloat16),
            pltpu.VMEM((2, strip_rows, 2, width), jnp.bfloat16),
            pltpu.VMEM((2, lat_rows, width), jnp.bfloat16),
            pltpu.SemaphoreType.DMA((4,)),
        ],
        compiler_params=params,
    )(*in_hbm(jnp.asarray(table), stale_pairs.transpose(1, 0, 2), step_pairs.transpose(0, 2, 1, 3), queries))

    def to(rows, flip):
        return lax.ppermute(rows, "patch", [(i, i ^ flip) for i in range(strips)])

    cores = lax.axis_size("head")
    partners = (across, across | across // 2)

    def to_partner(rows):
        pairs = [(i * cores + c, (i ^ partners[c % 2]) * cores + c) for i in range(strips) for c in range(cores)]
        return lax.ppermute(rows, ("patch", "head"), pairs)

    partner_query = to_partner(query)
    others = [to(block, flip) for flip in neighbours]
    bias, total, gates, weight = pl.pallas_call(
        fetch_kernel,
        out_shape=(f32((len(whose), columns)), f32((lat_rows, model)), f32((2, model)), bf16(out_weight.shape)),
        in_specs=[smem, vmem] + [hbm] * 4,
        out_specs=(vmem,) * 4,
        scratch_shapes=[
            pltpu.SMEM(t_index.shape, jnp.int32),
            pltpu.VMEM(gate_table.shape, jnp.bfloat16),
            pltpu.VMEM(hidden.shape, jnp.bfloat16),
            pltpu.SemaphoreType.DMA((3 + CHUNKS,)),
        ],
        compiler_params=params,
    )(text_len, mask, *in_hbm(t_index, gate_table, hidden, out_weight))
    partial_rows = pl.pallas_call(
        functools.partial(partner_kernel, query_rows),
        out_shape=bf16((query_rows, width + LANES)),
        in_specs=[vmem] * (4 + len(others)),
        out_specs=vmem,
        compiler_params=params,
    )(bias, block, local, partner_query, *others)
    mixed, logs = pl.pallas_call(
        functools.partial(own_kernel, query_rows),
        out_shape=(f32((query_rows, width)), f32((query_rows, LANES))),
        in_specs=[vmem] * (3 + len(others)),
        out_specs=(vmem,) * 2,
        compiler_params=params,
    )(bias, block, local, *others)
    partner_rows = to_partner(partial_rows)

    keep, send = pl.pallas_call(
        project_kernel,
        out_shape=(f32((lat_rows // 2, model)), bf16((lat_rows // 2, model))),
        in_specs=[vmem] * 6,
        out_specs=(vmem, vmem),
        compiler_params=params,
    )(mixed, logs, partner_rows, weight, gates, total)
    received = lax.ppermute(send, "head", [(0, 1), (1, 0)])
    return (keep + received.astype(jnp.float32)).astype(jnp.bfloat16)


def solution(mesh):
    return jax.shard_map(
        per_device,
        mesh=mesh,
        in_specs=(
            P(None, ("groups", "patch"), "head"),
            P(None, ("groups", "patch"), "head"),
            P(None, None, ("groups", "patch"), "head"),
            P(("groups", "patch"), "head"),
            P("head", None),
            P(),
            P("groups"),
            P("groups"),
        ),
        out_specs=P(("groups", "patch", "head"), None),
        check_vma=False,
    )
```

```python
import functools

import jax
import jax.numpy as jnp
import numpy as np
from jax import lax
from jax.experimental import pallas as pl
from jax.experimental.pallas import tpu as pltpu
from jax.sharding import PartitionSpec as P

HDIM = 128
LANES = 128
MASKED = -1e30
VMEM_LIMIT = 24 * 1024 * 1024
TERMS, TERM_LANES = 3, 32
CHUNKS = 6


def round_up(value, step):
    return (value + step - 1) // step * step


def pack_kernel(text_rows, table_hbm, stale_hbm, step_hbm, query_hbm, block_ref, local_ref, query_ref, mask_ref,
                table_ref, stale, step, query, sems):
    copies = [
        pltpu.make_async_copy(stale_hbm, stale, sems.at[0]),
        pltpu.make_async_copy(step_hbm, step, sems.at[1]),
        pltpu.make_async_copy(query_hbm, query, sems.at[2]),
        pltpu.make_async_copy(table_hbm, table_ref, sems.at[3]),
    ]
    for copy in copies:
        copy.start()
    for copy in copies:
        copy.wait()
    strip = lax.axis_index("patch")
    classes = mask_ref.shape[0] - 1
    early = table_ref[classes + 1 : classes + 2, :]
    mask_ref[:classes, :] = table_ref[:classes, :]
    mask_ref[classes:, :] = jnp.where(early < 0, -1, (strip ^ table_ref[classes : classes + 1, :]) * text_rows + early)
    width = block_ref.shape[1]
    block_ref[...] = jnp.concatenate([stale[...].reshape(-1, width), step[0].reshape(-1, width)], axis=0)
    query_ref[...] = query[...].reshape(-1, width)
    local_ref[...] = jnp.concatenate([query[...].reshape(-1, width), step[1].reshape(-1, width)], axis=0)


def blocks_of(ref):
    return [slice(i, i + HDIM) for i in range(0, ref.shape[-1], HDIM)]


def attention(query_rows, bias_ref, own_ref, local_ref, query_ref, others, first_class):
    columns = bias_ref.shape[1]
    bias = jnp.concatenate(
        [jnp.broadcast_to(bias_ref[first_class + c : first_class + c + 1, :], (query_rows // 2, columns)) for c in range(2)],
        axis=0,
    )
    lane_blocks = blocks_of(own_ref)
    rows, scores = [], []
    for lanes in lane_blocks:
        parts = [own_ref[:, lanes]] + [ref[:, lanes] for ref in others] + [local_ref[query_rows:, lanes]]
        filled = sum(part.shape[0] for part in parts)
        if filled < columns:
            parts.append(jnp.zeros((columns - filled, HDIM), jnp.bfloat16))
        rows.append(jnp.concatenate(parts, axis=0))
        scores.append(
            lax.dot_general(
                query_ref[:query_rows, lanes], rows[-1], (((1,), (1,)), ((), ())), preferred_element_type=jnp.float32
            )
            * (1.0 / HDIM**0.5)
            + bias
        )
    tops = [jnp.max(score, axis=1, keepdims=True) for score in scores]
    expos = [jnp.exp(score - top) for score, top in zip(scores, tops)]
    norms = [jnp.sum(expo, axis=1, keepdims=True) for expo in expos]
    sums = [
        jnp.dot(pltpu.roll(expo, 1, 1).astype(jnp.bfloat16), row, preferred_element_type=jnp.float32)
        for expo, row in zip(expos, rows)
    ]
    mixed = [whole * (1.0 / norm) for whole, norm in zip(sums, norms)]
    lane = lax.broadcasted_iota(jnp.int32, (query_rows, LANES), 1)
    all_norms, all_tops = jnp.ones((query_rows, LANES), jnp.float32), jnp.zeros((query_rows, LANES), jnp.float32)
    for head, (norm, top) in enumerate(zip(norms, tops)):
        all_norms = jnp.where(lane == head, norm, all_norms)
        all_tops = jnp.where(lane == head, top, all_tops)
    logs = all_tops + jnp.log(all_norms)
    return mixed, logs


def own_kernel(query_rows, bias_ref, own_ref, local_ref, *refs):
    others, (mixed_ref, log_ref) = refs[:-2], refs[-2:]
    mixed, logs = attention(query_rows, bias_ref, own_ref, local_ref, local_ref, others, 0)
    for lanes, rows in zip(blocks_of(own_ref), mixed):
        mixed_ref[:, lanes] = rows
    log_ref[...] = logs


def partner_kernel(query_rows, bias_ref, own_ref, local_ref, query_ref, *refs):
    others, partner_ref = refs[:-1], refs[-1]
    mixed, rest = attention(query_rows, bias_ref, own_ref, local_ref, query_ref, others, 2)
    for lanes, rows in zip(blocks_of(own_ref), mixed):
        partner_ref[:, lanes] = rows.astype(jnp.bfloat16)
    coded = jnp.zeros_like(rest)
    for term in range(TERMS):
        part = rest.astype(jnp.bfloat16).astype(jnp.float32)
        coded = coded + (pltpu.roll(part, term * TERM_LANES, 1) if term else part)
        rest = rest - part
    partner_ref[:, own_ref.shape[1] :] = coded.astype(jnp.bfloat16)


def decoded(packed, width):
    coded = packed[:, width:]
    logs = pltpu.roll(coded, LANES - 2 * TERM_LANES, 1) + pltpu.roll(coded, LANES - TERM_LANES, 1) + coded
    return packed[:, :width], logs


def joined(one, two, lane_blocks):
    (mixed, logs), (other_mixed, other_logs) = one, two
    parts = []
    for head, lanes in enumerate(lane_blocks):
        log, other_log = logs[:, head : head + 1], other_logs[:, head : head + 1]
        top = jnp.maximum(log, other_log)
        share, other_share = jnp.exp(log - top), jnp.exp(other_log - top)
        whole = share + other_share
        parts.append(mixed[:, lanes] * (share / whole) + other_mixed[:, lanes] * (other_share / whole))
    return jnp.concatenate(parts, axis=1).astype(jnp.bfloat16)


def fetch_kernel(text_ref, mask_ref, plan_hbm, table_hbm, hidden_hbm, weight_hbm, bias_ref, sum_ref, gates_ref, weight_ref,
                 plan_ref, table_ref, hidden_ref, sems):
    small = [
        pltpu.make_async_copy(plan_hbm, plan_ref, sems.at[0]),
        pltpu.make_async_copy(table_hbm, table_ref, sems.at[1]),
        pltpu.make_async_copy(hidden_hbm, hidden_ref, sems.at[2]),
    ]
    depth = weight_ref.shape[0] // CHUNKS
    large = [
        pltpu.make_async_copy(
            weight_hbm.at[pl.ds(chunk * depth, depth), :], weight_ref.at[pl.ds(chunk * depth, depth), :], sems.at[3 + chunk]
        )
        for chunk in range(CHUNKS)
    ]
    for copy in small + large:
        copy.start()
    classes = bias_ref.shape[0]
    live = mask_ref[classes:, :] < text_ref[0]
    bias_ref[...] = jnp.where((mask_ref[:classes, :] > 0) & live, 0.0, MASKED)
    for copy in small:
        copy.wait()
    table = table_ref[...].astype(jnp.float32)
    entry = lax.broadcasted_iota(jnp.int32, table.shape, 0)
    for step in range(2):
        row = jnp.sum(jnp.where(entry == plan_ref[step], table, 0.0), axis=0, keepdims=True)
        gates_ref[step : step + 1, :] = row
    width = hidden_ref.shape[1]
    lanes = pl.ds(pl.multiple_of(lax.axis_index("head") * width, LANES), width)
    sum_ref[...] = jnp.zeros_like(sum_ref)
    sum_ref[:, lanes] = hidden_ref[...].astype(jnp.float32)
    for copy in large:
        copy.wait()


def rows_of(rows, mine):
    part = rows.shape[0] // 4
    low = jnp.concatenate([rows[:part], rows[2 * part : 3 * part]], axis=0)
    high = jnp.concatenate([rows[part : 2 * part], rows[3 * part :]], axis=0)
    return jnp.where((lax.axis_index("head") == 0) == mine, low, high)


def project_kernel(mine, mixed_ref, log_ref, partner_ref, weight_ref, gates_ref, sum_ref, out_ref):
    half = out_ref.shape[0]
    own = rows_of(mixed_ref[...], mine), rows_of(log_ref[...], mine)
    partner = rows_of(partner_ref[...].astype(jnp.float32), mine)
    attended = joined(own, decoded(partner, mixed_ref.shape[1]), blocks_of(mixed_ref))
    projected = jnp.dot(attended, weight_ref[...], preferred_element_type=jnp.float32)
    base = jnp.where((lax.axis_index("head") == 0) == mine, sum_ref[:half, :], sum_ref[half:, :])
    total = base + gates_ref[0:1, :] * projected[:half] + gates_ref[1:2, :] * projected[half:]
    out_ref[...] = total.astype(out_ref.dtype)


def per_device(queries, stale_pairs, step_pairs, hidden, out_weight, gate_table, t_index, text_len):
    strips = lax.axis_size("patch")
    strip_rows = stale_pairs.shape[1]
    lat_rows = queries.shape[1]
    text_rows = strip_rows - lat_rows
    width = queries.shape[2]
    model = out_weight.shape[1]
    set_rows = 2 * strip_rows
    query_rows = 2 * lat_rows
    block_rows = 2 * set_rows
    smem = pl.BlockSpec(memory_space=pltpu.SMEM)
    vmem = pl.BlockSpec(memory_space=pltpu.VMEM)
    hbm = pl.BlockSpec(memory_space=pltpu.HBM)
    params = pltpu.CompilerParams(vmem_limit_bytes=VMEM_LIMIT)

    def in_hbm(*arrays):
        return [pltpu.with_memory_space_constraint(array, pltpu.HBM) for array in arrays]

    across = strips // 2
    neighbours = sorted(range(1, across), key=lambda flip: (-bin(flip).count("1"), flip))
    pieces = [(flip, kind) for flip in [0] + neighbours for kind in (0, 1)] + [(0, 2)]
    whose, step = np.asarray([0, 0, across, across])[:, None], np.asarray([0, 1, 0, 1])[:, None]
    columns = round_up(set_rows * len(pieces), LANES)
    column = np.arange(columns)
    within = column % set_rows
    flip, kind = np.asarray(pieces)[np.minimum(column // set_rows, len(pieces) - 1)].T
    is_key = (column < set_rows * len(pieces)) & (within % 2 == 0)
    chosen = is_key & (kind == np.where(flip == whose, step + 1, step))
    table = np.concatenate([chosen, flip[None], (within // 2 - lat_rows)[None]], axis=0).astype(np.int32)

    bf16 = functools.partial(jax.ShapeDtypeStruct, dtype=jnp.bfloat16)
    f32 = functools.partial(jax.ShapeDtypeStruct, dtype=jnp.float32)
    block, local, query, mask = pl.pallas_call(
        functools.partial(pack_kernel, text_rows),
        out_shape=(
            bf16((block_rows, width)),
            bf16((query_rows + set_rows, width)),
            bf16((query_rows, width)),
            jax.ShapeDtypeStruct((len(whose) + 1, columns), jnp.int32),
        ),
        in_specs=[hbm] * 4,
        out_specs=(vmem,) * 4,
        scratch_shapes=[
            pltpu.VMEM(table.shape, jnp.int32),
            pltpu.VMEM((strip_rows, 2, width), jnp.bfloat16),
            pltpu.VMEM((2, strip_rows, 2, width), jnp.bfloat16),
            pltpu.VMEM((2, lat_rows, width), jnp.bfloat16),
            pltpu.SemaphoreType.DMA((4,)),
        ],
        compiler_params=params,
    )(*in_hbm(jnp.asarray(table), stale_pairs.transpose(1, 0, 2), step_pairs.transpose(0, 2, 1, 3), queries))

    def to(rows, flip):
        return lax.ppermute(rows, "patch", [(i, i ^ flip) for i in range(strips)])

    cores = lax.axis_size("head")
    partners = (across, across | across // 2)

    def to_partner(rows):
        pairs = [(i * cores + c, (i ^ partners[c % 2]) * cores + c) for i in range(strips) for c in range(cores)]
        return lax.ppermute(rows, ("patch", "head"), pairs)

    partner_query = to_partner(query)
    others = [to(block, flip) for flip in neighbours]
    bias, total, gates, weight = pl.pallas_call(
        fetch_kernel,
        out_shape=(f32((len(whose), columns)), f32((lat_rows, model)), f32((2, model)), bf16(out_weight.shape)),
        in_specs=[smem, vmem] + [hbm] * 4,
        out_specs=(vmem,) * 4,
        scratch_shapes=[
            pltpu.SMEM(t_index.shape, jnp.int32),
            pltpu.VMEM(gate_table.shape, jnp.bfloat16),
            pltpu.VMEM(hidden.shape, jnp.bfloat16),
            pltpu.SemaphoreType.DMA((3 + CHUNKS,)),
        ],
        compiler_params=params,
    )(text_len, mask, *in_hbm(t_index, gate_table, hidden, out_weight))
    partial_rows = pl.pallas_call(
        functools.partial(partner_kernel, query_rows),
        out_shape=bf16((query_rows, width + LANES)),
        in_specs=[vmem] * (4 + len(others)),
        out_specs=vmem,
        compiler_params=params,
    )(bias, block, local, partner_query, *others)
    mixed, logs = pl.pallas_call(
        functools.partial(own_kernel, query_rows),
        out_shape=(f32((query_rows, width)), f32((query_rows, LANES))),
        in_specs=[vmem] * (3 + len(others)),
        out_specs=(vmem,) * 2,
        compiler_params=params,
    )(bias, block, local, *others)
    partner_rows = to_partner(partial_rows)

    def project(mine, dtype):
        return pl.pallas_call(
            functools.partial(project_kernel, mine),
            out_shape=jax.ShapeDtypeStruct((lat_rows // 2, model), dtype),
            in_specs=[vmem] * 6,
            out_specs=vmem,
            compiler_params=params,
        )(mixed, logs, partner_rows, weight, gates, total)

    send, keep = project(False, jnp.bfloat16), project(True, jnp.float32)
    received = lax.ppermute(send, "head", [(0, 1), (1, 0)])
    return (keep + received.astype(jnp.float32)).astype(jnp.bfloat16)


def solution(mesh):
    return jax.shard_map(
        per_device,
        mesh=mesh,
        in_specs=(
            P(None, ("groups", "patch"), "head"),
            P(None, ("groups", "patch"), "head"),
            P(None, None, ("groups", "patch"), "head"),
            P(("groups", "patch"), "head"),
            P("head", None),
            P(),
            P("groups"),
            P("groups"),
        ),
        out_specs=P(("groups", "patch", "head"), None),
        check_vma=False,
    )
```

```python
import functools

import jax
import jax.numpy as jnp
import numpy as np
from jax import lax
from jax.experimental import pallas as pl
from jax.experimental.pallas import tpu as pltpu
from jax.sharding import PartitionSpec as P

HDIM = 128
LANES = 128
MASKED = -1e30
VMEM_LIMIT = 24 * 1024 * 1024
TERMS, TERM_LANES = 3, 32
CHUNKS = 4


def round_up(value, step):
    return (value + step - 1) // step * step


def pack_kernel(text_rows, table_hbm, stale_hbm, step_hbm, query_hbm, block_ref, local_ref, query_ref, mask_ref,
                table_ref, stale, step, query, sems):
    copies = [
        pltpu.make_async_copy(stale_hbm, stale, sems.at[0]),
        pltpu.make_async_copy(step_hbm, step, sems.at[1]),
        pltpu.make_async_copy(query_hbm, query, sems.at[2]),
        pltpu.make_async_copy(table_hbm, table_ref, sems.at[3]),
    ]
    for copy in copies:
        copy.start()
    for copy in copies:
        copy.wait()
    strip = lax.axis_index("patch")
    classes = mask_ref.shape[0] - 1
    early = table_ref[classes + 1 : classes + 2, :]
    mask_ref[:classes, :] = table_ref[:classes, :]
    mask_ref[classes:, :] = jnp.where(early < 0, -1, (strip ^ table_ref[classes : classes + 1, :]) * text_rows + early)
    width = block_ref.shape[1]
    block_ref[...] = jnp.concatenate([stale[...].reshape(-1, width), step[0].reshape(-1, width)], axis=0)
    query_ref[...] = query[...].reshape(-1, width)
    local_ref[...] = jnp.concatenate([query[...].reshape(-1, width), step[1].reshape(-1, width)], axis=0)


def blocks_of(ref):
    return [slice(i, i + HDIM) for i in range(0, ref.shape[-1], HDIM)]


def attention(query_rows, bias_ref, own_ref, local_ref, query_ref, others, first_class):
    columns = bias_ref.shape[1]
    bias = jnp.concatenate(
        [jnp.broadcast_to(bias_ref[first_class + c : first_class + c + 1, :], (query_rows // 2, columns)) for c in range(2)],
        axis=0,
    )
    lane_blocks = blocks_of(own_ref)
    rows, scores = [], []
    for lanes in lane_blocks:
        parts = [own_ref[:, lanes]] + [ref[:, lanes] for ref in others] + [local_ref[query_rows:, lanes]]
        filled = sum(part.shape[0] for part in parts)
        if filled < columns:
            parts.append(jnp.zeros((columns - filled, HDIM), jnp.bfloat16))
        rows.append(jnp.concatenate(parts, axis=0))
        scores.append(
            lax.dot_general(
                query_ref[:query_rows, lanes], rows[-1], (((1,), (1,)), ((), ())), preferred_element_type=jnp.float32
            )
            * (1.0 / HDIM**0.5)
            + bias
        )
    tops = [jnp.max(score, axis=1, keepdims=True) for score in scores]
    expos = [jnp.exp(score - top) for score, top in zip(scores, tops)]
    norms = [jnp.sum(expo, axis=1, keepdims=True) for expo in expos]
    sums = [
        jnp.dot(pltpu.roll(expo, 1, 1).astype(jnp.bfloat16), row, preferred_element_type=jnp.float32)
        for expo, row in zip(expos, rows)
    ]
    mixed = [whole * (1.0 / norm) for whole, norm in zip(sums, norms)]
    lane = lax.broadcasted_iota(jnp.int32, (query_rows, LANES), 1)
    all_norms, all_tops = jnp.ones((query_rows, LANES), jnp.float32), jnp.zeros((query_rows, LANES), jnp.float32)
    for head, (norm, top) in enumerate(zip(norms, tops)):
        all_norms = jnp.where(lane == head, norm, all_norms)
        all_tops = jnp.where(lane == head, top, all_tops)
    logs = all_tops + jnp.log(all_norms)
    return mixed, logs


def own_kernel(query_rows, bias_ref, own_ref, local_ref, *refs):
    others, (mixed_ref, log_ref) = refs[:-2], refs[-2:]
    mixed, logs = attention(query_rows, bias_ref, own_ref, local_ref, local_ref, others, 0)
    for lanes, rows in zip(blocks_of(own_ref), mixed):
        mixed_ref[:, lanes] = rows
    log_ref[...] = logs


def partner_kernel(query_rows, bias_ref, own_ref, local_ref, query_ref, *refs):
    others, partner_ref = refs[:-1], refs[-1]
    mixed, rest = attention(query_rows, bias_ref, own_ref, local_ref, query_ref, others, 2)
    for lanes, rows in zip(blocks_of(own_ref), mixed):
        partner_ref[:, lanes] = rows.astype(jnp.bfloat16)
    coded = jnp.zeros_like(rest)
    for term in range(TERMS):
        part = rest.astype(jnp.bfloat16).astype(jnp.float32)
        coded = coded + (pltpu.roll(part, term * TERM_LANES, 1) if term else part)
        rest = rest - part
    partner_ref[:, own_ref.shape[1] :] = coded.astype(jnp.bfloat16)


def decoded(packed, width):
    coded = packed[:, width:]
    logs = pltpu.roll(coded, LANES - 2 * TERM_LANES, 1) + pltpu.roll(coded, LANES - TERM_LANES, 1) + coded
    return packed[:, :width], logs


def joined(one, two, lane_blocks):
    (mixed, logs), (other_mixed, other_logs) = one, two
    parts = []
    for head, lanes in enumerate(lane_blocks):
        log, other_log = logs[:, head : head + 1], other_logs[:, head : head + 1]
        top = jnp.maximum(log, other_log)
        share, other_share = jnp.exp(log - top), jnp.exp(other_log - top)
        whole = share + other_share
        parts.append(mixed[:, lanes] * (share / whole) + other_mixed[:, lanes] * (other_share / whole))
    return jnp.concatenate(parts, axis=1).astype(jnp.bfloat16)


def fetch_kernel(text_ref, mask_ref, plan_hbm, table_hbm, hidden_hbm, weight_hbm, bias_ref, sum_ref, gates_ref, weight_ref,
                 plan_ref, table_ref, hidden_ref, sems):
    small = [
        pltpu.make_async_copy(plan_hbm, plan_ref, sems.at[0]),
        pltpu.make_async_copy(table_hbm, table_ref, sems.at[1]),
        pltpu.make_async_copy(hidden_hbm, hidden_ref, sems.at[2]),
    ]
    depth = weight_ref.shape[0] // CHUNKS
    large = [
        pltpu.make_async_copy(
            weight_hbm.at[pl.ds(chunk * depth, depth), :], weight_ref.at[pl.ds(chunk * depth, depth), :], sems.at[3 + chunk]
        )
        for chunk in range(CHUNKS)
    ]
    for copy in small + large:
        copy.start()
    classes = bias_ref.shape[0]
    live = mask_ref[classes:, :] < text_ref[0]
    bias_ref[...] = jnp.where((mask_ref[:classes, :] > 0) & live, 0.0, MASKED)
    for copy in small:
        copy.wait()
    table = table_ref[...].astype(jnp.float32)
    entry = lax.broadcasted_iota(jnp.int32, table.shape, 0)
    for step in range(2):
        row = jnp.sum(jnp.where(entry == plan_ref[step], table, 0.0), axis=0, keepdims=True)
        gates_ref[step : step + 1, :] = row
    width = hidden_ref.shape[1]
    lanes = pl.ds(pl.multiple_of(lax.axis_index("head") * width, LANES), width)
    sum_ref[...] = jnp.zeros_like(sum_ref)
    sum_ref[:, lanes] = hidden_ref[...].astype(jnp.float32)
    for copy in large:
        copy.wait()


def rows_of(rows, mine):
    part = rows.shape[0] // 4
    low = jnp.concatenate([rows[:part], rows[2 * part : 3 * part]], axis=0)
    high = jnp.concatenate([rows[part : 2 * part], rows[3 * part :]], axis=0)
    return jnp.where((lax.axis_index("head") == 0) == mine, low, high)


def fetch_rest_kernel(_, weight_hbm, weight_ref, sems):
    rows = weight_ref.shape[0]
    depth = rows // CHUNKS
    copies = [
        pltpu.make_async_copy(
            weight_hbm.at[pl.ds(rows + chunk * depth, depth), :], weight_ref.at[pl.ds(chunk * depth, depth), :], sems.at[chunk]
        )
        for chunk in range(CHUNKS)
    ]
    for copy in copies:
        copy.start()
    for copy in copies:
        copy.wait()


def project_kernel(mine, mixed_ref, log_ref, partner_ref, weight_ref, rest_ref, gates_ref, sum_ref, out_ref):
    half = out_ref.shape[0]
    own = rows_of(mixed_ref[...], mine), rows_of(log_ref[...], mine)
    partner = rows_of(partner_ref[...].astype(jnp.float32), mine)
    attended = joined(own, decoded(partner, mixed_ref.shape[1]), blocks_of(mixed_ref))
    depth = weight_ref.shape[0]
    projected = jnp.dot(attended[:, :depth], weight_ref[...], preferred_element_type=jnp.float32)
    projected += jnp.dot(attended[:, depth:], rest_ref[...], preferred_element_type=jnp.float32)
    base = jnp.where((lax.axis_index("head") == 0) == mine, sum_ref[:half, :], sum_ref[half:, :])
    total = base + gates_ref[0:1, :] * projected[:half] + gates_ref[1:2, :] * projected[half:]
    out_ref[...] = total.astype(out_ref.dtype)


def per_device(queries, stale_pairs, step_pairs, hidden, out_weight, gate_table, t_index, text_len):
    strips = lax.axis_size("patch")
    strip_rows = stale_pairs.shape[1]
    lat_rows = queries.shape[1]
    text_rows = strip_rows - lat_rows
    width = queries.shape[2]
    model = out_weight.shape[1]
    set_rows = 2 * strip_rows
    query_rows = 2 * lat_rows
    block_rows = 2 * set_rows
    smem = pl.BlockSpec(memory_space=pltpu.SMEM)
    vmem = pl.BlockSpec(memory_space=pltpu.VMEM)
    hbm = pl.BlockSpec(memory_space=pltpu.HBM)
    params = pltpu.CompilerParams(vmem_limit_bytes=VMEM_LIMIT)

    def in_hbm(*arrays):
        return [pltpu.with_memory_space_constraint(array, pltpu.HBM) for array in arrays]

    across = strips // 2
    neighbours = sorted(range(1, across), key=lambda flip: (-bin(flip).count("1"), flip))
    pieces = [(flip, kind) for flip in [0] + neighbours for kind in (0, 1)] + [(0, 2)]
    whose, step = np.asarray([0, 0, across, across])[:, None], np.asarray([0, 1, 0, 1])[:, None]
    columns = round_up(set_rows * len(pieces), LANES)
    column = np.arange(columns)
    within = column % set_rows
    flip, kind = np.asarray(pieces)[np.minimum(column // set_rows, len(pieces) - 1)].T
    is_key = (column < set_rows * len(pieces)) & (within % 2 == 0)
    chosen = is_key & (kind == np.where(flip == whose, step + 1, step))
    table = np.concatenate([chosen, flip[None], (within // 2 - lat_rows)[None]], axis=0).astype(np.int32)

    bf16 = functools.partial(jax.ShapeDtypeStruct, dtype=jnp.bfloat16)
    f32 = functools.partial(jax.ShapeDtypeStruct, dtype=jnp.float32)
    block, local, query, mask = pl.pallas_call(
        functools.partial(pack_kernel, text_rows),
        out_shape=(
            bf16((block_rows, width)),
            bf16((query_rows + set_rows, width)),
            bf16((query_rows, width)),
            jax.ShapeDtypeStruct((len(whose) + 1, columns), jnp.int32),
        ),
        in_specs=[hbm] * 4,
        out_specs=(vmem,) * 4,
        scratch_shapes=[
            pltpu.VMEM(table.shape, jnp.int32),
            pltpu.VMEM((strip_rows, 2, width), jnp.bfloat16),
            pltpu.VMEM((2, strip_rows, 2, width), jnp.bfloat16),
            pltpu.VMEM((2, lat_rows, width), jnp.bfloat16),
            pltpu.SemaphoreType.DMA((4,)),
        ],
        compiler_params=params,
    )(*in_hbm(jnp.asarray(table), stale_pairs.transpose(1, 0, 2), step_pairs.transpose(0, 2, 1, 3), queries))

    def to(rows, flip):
        return lax.ppermute(rows, "patch", [(i, i ^ flip) for i in range(strips)])

    cores = lax.axis_size("head")
    partners = (across, across | across // 2)

    def to_partner(rows):
        pairs = [(i * cores + c, (i ^ partners[c % 2]) * cores + c) for i in range(strips) for c in range(cores)]
        return lax.ppermute(rows, ("patch", "head"), pairs)

    partner_query = to_partner(query)
    others = [to(block, flip) for flip in neighbours]
    bias, total, gates, weight = pl.pallas_call(
        fetch_kernel,
        out_shape=(f32((len(whose), columns)), f32((lat_rows, model)), f32((2, model)), bf16((width // 2, model))),
        in_specs=[smem, vmem] + [hbm] * 4,
        out_specs=(vmem,) * 4,
        scratch_shapes=[
            pltpu.SMEM(t_index.shape, jnp.int32),
            pltpu.VMEM(gate_table.shape, jnp.bfloat16),
            pltpu.VMEM(hidden.shape, jnp.bfloat16),
            pltpu.SemaphoreType.DMA((3 + CHUNKS,)),
        ],
        compiler_params=params,
    )(text_len, mask, *in_hbm(t_index, gate_table, hidden, out_weight))
    partial_rows = pl.pallas_call(
        functools.partial(partner_kernel, query_rows),
        out_shape=bf16((query_rows, width + LANES)),
        in_specs=[vmem] * (4 + len(others)),
        out_specs=vmem,
        compiler_params=params,
    )(bias, block, local, partner_query, *others)
    mixed, logs = pl.pallas_call(
        functools.partial(own_kernel, query_rows),
        out_shape=(f32((query_rows, width)), f32((query_rows, LANES))),
        in_specs=[vmem] * (3 + len(others)),
        out_specs=(vmem,) * 2,
        compiler_params=params,
    )(bias, block, local, *others)
    partner_rows = to_partner(partial_rows)

    rest = pl.pallas_call(
        fetch_rest_kernel,
        out_shape=bf16((width // 2, model)),
        in_specs=[vmem, hbm],
        out_specs=vmem,
        scratch_shapes=[pltpu.SemaphoreType.DMA((CHUNKS,))],
        compiler_params=params,
    )(logs, *in_hbm(out_weight))

    def project(mine, dtype):
        return pl.pallas_call(
            functools.partial(project_kernel, mine),
            out_shape=jax.ShapeDtypeStruct((lat_rows // 2, model), dtype),
            in_specs=[vmem] * 7,
            out_specs=vmem,
            compiler_params=params,
        )(mixed, logs, partner_rows, weight, rest, gates, total)

    send, keep = project(False, jnp.bfloat16), project(True, jnp.float32)
    received = lax.ppermute(send, "head", [(0, 1), (1, 0)])
    return (keep + received.astype(jnp.float32)).astype(jnp.bfloat16)


def solution(mesh):
    return jax.shard_map(
        per_device,
        mesh=mesh,
        in_specs=(
            P(None, ("groups", "patch"), "head"),
            P(None, ("groups", "patch"), "head"),
            P(None, None, ("groups", "patch"), "head"),
            P(("groups", "patch"), "head"),
            P("head", None),
            P(),
            P("groups"),
            P("groups"),
        ),
        out_specs=P(("groups", "patch", "head"), None),
        check_vma=False,
    )
```
